256 devices in a mesh: ent: 32 (over y, x, core), rel: 8 (over z).
Axes of the slice: x: 4, y: 4, z: 8, core: 2. Of those that a mesh axis runs over, the one named last changes fastest.
Arguments:
- tile_vals: bfloat16 [32, 8, 64, 128, 128], P('ent', 'rel'), may hold values from -192 to 192
- tile_row: int32 [32, 8, 64], P('ent', 'rel'), may hold values from 0 to 3
- tile_rel: int32 [32, 8, 64], P('ent', 'rel'), may hold values from 0 to 1
- tile_src: int32 [32, 8, 64], P('ent', 'rel'), may hold values from 0 to 31
- needed: int32 [32, 8, 32, 1], P('ent', 'rel'), may hold values from 0 to 3
- factors: bfloat16 [16384, 256], P('ent'), may hold values from -6 to 6
- cores: bfloat16 [16, 256, 256], P('rel'), may hold values from -0.5 to 1.5
- basis: float32 [256, 256], replicated, may hold values from -1 to 1
- spectrum: float32 [256], replicated, may hold values from 100 to 1000
Outputs:
- new_factors: bfloat16 [16384, 256], P('ent')
- new_cores: float32 [16, 256, 256], P('rel')
The draws below stay inside these ranges and needn't reach their ends.
Inputs may be any that keep to these rules, and one draw needn't show every extreme that they name: tile_src names the owner whose single requested block (slot 0 of `needed`) gives the tile's columns. `needed`: every request slot names a block.
All inputs are finite; a program needn't handle non-finite values.
Results may differ from the reference program's by a relative error of at most 0.0081.
Values may be sent and summed in bfloat16 or wider, within the bound.
A program may use at most 64 MiB of HBM per device.

```python
import math
import jax
import jax.numpy as jnp
import numpy as np
from jax import lax

R = 256
BLK = 128
CAP = 1
E_DEV = 512
TILES = 64
REL_DEV = 2
NE = 16384
K = 16
N_ENT = 32
N_REL = 8


def draw_factors(key, part):
    key = jax.random.fold_in(key, 11)
    key_base, key_rows, key_cols = jax.random.split(key, 3)
    positions = jnp.arange(NE, dtype=jnp.float32)
    row_ramp = jnp.exp(math.log(3.0) * positions / NE)[:, None]
    col_scale = jnp.exp(jax.random.uniform(key_cols, (1, R), jnp.float32, 0.0, math.log(3.0)))
    values = jnp.clip(jax.random.normal(key_base, (NE, R), jnp.float32), -4.0, 4.0)
    row_scale = jnp.exp(jax.random.uniform(key_rows, (NE, 1), jnp.float32, 0.0, math.log(4.0)))
    return (0.015 * values * row_scale * col_scale * row_ramp).astype(jnp.bfloat16)


def draw_cores(key, part):
    key = jax.random.fold_in(key, 23)
    key_diag, key_off = jax.random.split(key, 2)
    identity = jnp.eye(R, dtype=jnp.float32)
    diagonal = 1.0 + jax.random.uniform(key_diag, (K, R, 1), jnp.float32, -0.2, 0.2)
    spread = jnp.clip(jax.random.normal(key_off, (K, R, R), jnp.float32), -4.0, 4.0)
    return (identity[None] * diagonal + 0.6 / math.sqrt(R) * spread).astype(jnp.bfloat16)


def draw_basis(key, part):
    key = jax.random.fold_in(key, 37)
    key_perm, key_sign = jax.random.split(key, 2)
    freqs = jax.random.permutation(key_perm, R).astype(jnp.float32)[:, None]
    signs = (2 * jax.random.randint(key_sign, (1, R), 0, 2) - 1).astype(jnp.float32)
    columns = jnp.arange(R, dtype=jnp.float32)[None, :]
    norms = jnp.where(freqs == 0.0, math.sqrt(1.0 / R), math.sqrt(2.0 / R))
    return norms * jnp.cos(math.pi * (2.0 * columns + 1.0) * freqs / (2.0 * R)) * signs


def place_ends(result, rng, least, high):
    longest = result.shape.index(max(result.shape))
    spots = []
    for shift in (0, 1):
        where = [jax.random.randint(jax.random.fold_in(rng, axis), (), 0, length) for axis, length in enumerate(result.shape)]
        where[longest] = (where[longest] + shift) % result.shape[longest]
        spots.append(tuple(where))
    return result.at[spots[0]].set(least).at[spots[1]].set(high)


def block_scale(stream_key, extent, pieces, least, largest):
    loudness = 1.0
    for dim, parts in pieces:
        draws = jax.random.uniform(jax.random.fold_in(jax.random.fold_in(stream_key, 6), dim), (parts,), jnp.float32, least / len(pieces), largest / len(pieces))
        loudness = loudness * jnp.repeat(jnp.exp(draws), extent[dim] // parts).reshape((-1,) + (1,) * (len(extent) - 1 - dim))
    return loudness


def cumulative_ranks(count, slope):
    weights = [(1 << 20) // math.isqrt(standing ** slope) + 1 for standing in range(1, count + 1)]
    scale = 1 + sum(weights) // (1 << 30)
    return np.cumsum(np.array([max(1, weight // scale) for weight in weights]))


def ranked(own_key, dims, count, skew):
    grid = cumulative_ranks(count, skew)
    ticket = jax.random.randint(jax.random.fold_in(own_key, 1), dims, 0, int(grid[count - 1]))
    rank = jnp.searchsorted(jnp.asarray(grid, jnp.int32), ticket, side="right")
    return jax.random.permutation(jax.random.fold_in(own_key, 2), count)[rank].astype(jnp.int32)


def centred(rng, extent, width, most, cuts=(), kind=jnp.bfloat16):
    array = width * jax.random.normal(rng, extent, jnp.float32)
    if cuts:
        array = array * block_scale(rng, extent, cuts, -0.22, 0.18)
    return jnp.clip(array, -most, most).astype(kind)


def setup_inputs(seed: int = 0) -> dict:
    seeds = jax.random.split(jax.random.key(seed), 10)
    tile_vals = centred(seeds[0], (N_ENT, N_REL, TILES, BLK, BLK), 32.0, 192.0, ((0, 32), (1, 8)))
    tile_row = place_ends(jax.random.randint(seeds[1], (N_ENT, N_REL, TILES), 0, E_DEV // BLK), jax.random.fold_in(seeds[1], 1), 0, (E_DEV // BLK) - 1).astype(jnp.int32)
    tile_rel = place_ends(jax.random.randint(seeds[2], (N_ENT, N_REL, TILES), 0, REL_DEV), jax.random.fold_in(seeds[2], 1), 0, REL_DEV - 1).astype(jnp.int32)
    tile_src = place_ends(ranked(seeds[3], (N_ENT, N_REL, TILES), N_ENT * CAP, 2), jax.random.fold_in(seeds[3], 3), 0, (N_ENT * CAP) - 1).astype(jnp.int32)
    needed = place_ends(jax.random.randint(seeds[4], (N_ENT, N_REL, N_ENT, CAP), 0, E_DEV // BLK), jax.random.fold_in(seeds[4], 1), 0, (E_DEV // BLK) - 1).astype(jnp.int32)
    factors = draw_factors(jax.random.fold_in(seeds[9], 71), 0)
    cores = draw_cores(jax.random.fold_in(seeds[9], 71), 0)
    basis = draw_basis(jax.random.fold_in(seeds[9], 71), 0)
    spectrum = jnp.clip(jnp.exp(jax.random.uniform(seeds[8], (R,), jnp.float32, math.log(100.0), math.log(1000.0))), 100.0, 1000.0)
    return dict(tile_vals=tile_vals, tile_row=tile_row, tile_rel=tile_rel, tile_src=tile_src, needed=needed, factors=factors, cores=cores, basis=basis, spectrum=spectrum)


def grouped_sum(part_data, key_ids, group_count):
    onehot = (key_ids[:, None] == jnp.arange(group_count, dtype=jnp.int32)[None, :]).astype(jnp.float32)
    return jnp.einsum('tg,tar->gar', onehot, part_data.astype(jnp.float32), precision=lax.Precision.HIGHEST).astype(jnp.bfloat16)

def reference(tile_vals, tile_row, tile_rel, tile_src, needed, factors, cores, basis, spectrum):
    precise = lax.Precision.HIGHEST
    row_blocks = E_DEV // BLK
    slot_total = N_ENT * CAP
    block_total = NE // BLK
    core_f32 = cores.astype(jnp.float32)
    gram_total = jnp.dot(factors.T.astype(jnp.float32), factors.astype(jnp.float32), preferred_element_type=jnp.float32)
    system = jnp.einsum('kab,bc,kdc->ad', core_f32, gram_total, core_f32, precision=precise)
    system = system + jnp.einsum('kba,bc,kcd->ad', core_f32, gram_total, core_f32, precision=precise)
    system = system + jnp.eye(R, dtype=jnp.float32)
    old_blocks = factors.reshape(block_total, BLK, R)

    def device_view(step_index):
        ent_index = (step_index // N_REL).astype(jnp.int32)
        rel_index = (step_index % N_REL).astype(jnp.int32)
        tile_data = tile_vals[ent_index, rel_index].astype(jnp.float32)
        tile_rows = tile_row[ent_index, rel_index]
        tile_rels = tile_rel[ent_index, rel_index]
        sources = tile_src[ent_index, rel_index]
        asked_rows = needed[ent_index, rel_index]
        owners = sources // CAP
        col_block = (owners * row_blocks + asked_rows[owners, sources % CAP]).astype(jnp.int32)
        local_cores = lax.dynamic_slice(core_f32, (rel_index * REL_DEV, jnp.int32(0), jnp.int32(0)), (REL_DEV, R, R))
        return (ent_index, rel_index, tile_data, tile_rows, tile_rels, sources, asked_rows, col_block, local_cores)

    def forward_pass(step_index, numerator):
        ent_index, rel_index, tile_data, tile_rows, tile_rels, sources, asked_rows, col_block, local_cores = device_view(step_index)
        left_part = jnp.einsum('tab,tbr->tar', tile_data, old_blocks[col_block].astype(jnp.float32), precision=precise).astype(jnp.bfloat16)
        forward = grouped_sum(left_part, tile_rels * row_blocks + tile_rows, REL_DEV * row_blocks).reshape(REL_DEV, row_blocks, BLK, R)
        forward_term = jnp.einsum('kbar,ksr->bas', forward.astype(jnp.float32), local_cores, precision=precise)
        start = (ent_index * row_blocks).astype(jnp.int32)
        own_blocks = lax.dynamic_slice(old_blocks, (start, jnp.int32(0), jnp.int32(0)), (row_blocks, BLK, R))
        right_part = jnp.einsum('tab,tar->tbr', tile_data, own_blocks[tile_rows].astype(jnp.float32), precision=precise).astype(jnp.bfloat16)
        backward = grouped_sum(right_part, sources * REL_DEV + tile_rels, slot_total * REL_DEV).reshape(slot_total, REL_DEV, BLK, R)
        backward_term = jnp.einsum('skbr,krq->sbq', backward.astype(jnp.float32), local_cores, precision=precise)
        slot_ids = jnp.arange(slot_total, dtype=jnp.int32)
        targets = (slot_ids // CAP * row_blocks + asked_rows[slot_ids // CAP, slot_ids % CAP]).astype(jnp.int32)
        numerator = numerator.at[targets].add(backward_term)
        current = lax.dynamic_slice(numerator, (start, jnp.int32(0), jnp.int32(0)), (row_blocks, BLK, R))
        return lax.dynamic_update_slice(numerator, current + forward_term, (start, jnp.int32(0), jnp.int32(0)))
    numerator = lax.fori_loop(0, N_ENT * N_REL, forward_pass, jnp.zeros((block_total, BLK, R), jnp.float32))
    factor_low = jnp.linalg.cholesky(system)
    new_factors = jax.scipy.linalg.cho_solve((factor_low, True), numerator.reshape(NE, R).T).T.astype(jnp.bfloat16)
    new_blocks = new_factors.reshape(block_total, BLK, R)

    def core_pass(step_index, totals):
        ent_index, rel_index, tile_data, tile_rows, tile_rels, sources, asked_rows, col_block, local_cores = device_view(step_index)
        latest = jnp.einsum('tab,tbr->tar', tile_data, new_blocks[col_block].astype(jnp.float32), precision=precise).astype(jnp.bfloat16)
        summed = grouped_sum(latest, tile_rels * row_blocks + tile_rows, REL_DEV * row_blocks).reshape(REL_DEV, row_blocks, BLK, R)
        start = (ent_index * row_blocks).astype(jnp.int32)
        own_new = lax.dynamic_slice(new_blocks, (start, jnp.int32(0), jnp.int32(0)), (row_blocks, BLK, R))
        core_part = jnp.einsum('bar,kbas->krs', own_new.astype(jnp.float32), summed.astype(jnp.float32), precision=precise)
        first = (rel_index * REL_DEV).astype(jnp.int32)
        current = lax.dynamic_slice(totals, (first, jnp.int32(0), jnp.int32(0)), (REL_DEV, R, R))
        return lax.dynamic_update_slice(totals, current + core_part, (first, jnp.int32(0), jnp.int32(0)))
    totals = lax.fori_loop(0, N_ENT * N_REL, core_pass, jnp.zeros((K, R, R), jnp.float32))
    rotated = jnp.einsum('ri,krs,sj->kij', basis, totals, basis, precision=precise)
    weights = 1.0 / (spectrum[:, None] * spectrum[None, :] + 1.0)
    new_cores = jnp.einsum('ir,krs,js->kij', basis, weights[None] * rotated, basis, precision=precise)
    return (new_factors, new_cores)
```

```python
import functools
import jax
import jax.numpy as jnp
from jax import lax
from jax.experimental import pallas as pl
from jax.experimental.pallas import tpu as pltpu
from jax.sharding import PartitionSpec as P

ridge_shift = 1.0
N_ENT, N_REL = 32, 8
BLK, R, ROWS, TILES, REL_DEV, SLAB = 128, 256, 4, 64, 2, 512
HALF = SLAB // 2
MESH = pl.DeviceIdType.MESH
F32, BF16 = jnp.float32, jnp.bfloat16
HIGH = lax.Precision.HIGHEST
SPOT = {0: 0, -1: 1, 1: 2, 2: 3}


def dot(a, b, dims=((1,), (0,)), precision=None):
    return lax.dot_general(a, b, (dims, ((), ())), precision=precision, preferred_element_type=F32)


def send(src, dst, send_sem, recv_sem, target):
    return pltpu.make_async_remote_copy(
        src_ref=src, dst_ref=dst, send_sem=send_sem, recv_sem=recv_sem, device_id=target, device_id_type=MESH
    )


def wait_bytes(ref, sem):
    pltpu.make_async_copy(ref, ref, sem).wait()


def greet(me_ent, me_rel):
    barrier = pltpu.get_barrier_semaphore()

    def ent_signal(k, carry):
        pl.semaphore_signal(barrier, inc=1, device_id={"ent": lax.rem(me_ent + k, N_ENT)}, device_id_type=MESH)
        return carry

    def rel_signal(k, carry):
        pl.semaphore_signal(barrier, inc=1, device_id={"rel": lax.rem(me_rel + k, N_REL)}, device_id_type=MESH)
        return carry

    lax.fori_loop(1, N_ENT, ent_signal, 0)
    lax.fori_loop(1, N_REL, rel_signal, 0)
    pl.semaphore_wait(barrier, N_ENT + N_REL - 2)


def spread(axis, count, me, source_at, landing, send_sem, recv_sem):
    def one(k, carry):
        other = lax.rem(me + k, count)
        send(source_at(other), landing.at[me], send_sem, recv_sem, {axis: other}).start()
        return carry

    lax.fori_loop(1, count, one, 0)


def spread_wait(count, landing, source, send_sem, recv_sem):
    wait_bytes(landing.at[pl.ds(0, count - 1)], recv_sem)
    wait_bytes(landing.at[pl.ds(0, count - 1)], send_sem)


def ring_gather(me, own, table, send_sem, recv_sem):
    core = lax.rem(me, 2)
    col = lax.rem(me // 2, 4)
    row = me // 8
    way = 1 - 2 * core
    sibling = me + way

    def at(h, u, v):
        du, dv = (u, v) if h == 0 else (v, u)
        x = lax.rem(col + du * way + 8, 4)
        y = lax.rem(row + dv * way + 8, 4)
        return (y * 4 + x) * 2 + core

    def part(ref, h):
        return ref.at[pl.ds(h * HALF, HALF)]

    def go(h, u, v, target):
        slab = at(h, u, v)
        dst = part(table.at[slab], h)
        src = part(own, h) if (u, v) == (0, 0) else dst
        send(src, dst, send_sem, recv_sem.at[h, slab], {"ent": target}).start()

    def arrive(h, slab):
        dst = part(table.at[slab], h)
        pltpu.make_async_copy(dst, dst, recv_sem.at[h, slab]).wait()

    def first(h):
        go(h, 0, 0, at(h, 1, 0))
        go(h, 0, 0, at(h, -1, 0))
        go(h, 0, 0, at(h, 0, 1))
        go(h, 0, 0, at(h, 0, -1))
        go(h, 0, 0, sibling)

    def along_u(h, u):
        arrive(h, at(h, u, 0))
        if u == -1:
            go(h, u, 0, at(h, 1, 0))
        go(h, u, 0, at(h, 0, 1))
        go(h, u, 0, at(h, 0, -1))
        go(h, u, 0, sibling)

    def along_v(h, u, v):
        arrive(h, at(h, u, v))
        if v == -1:
            go(h, u, v, at(h, 0, 1))
        go(h, u, v, sibling)

    def both(act, *where):
        return lambda: [act(h, *where) for h in (0, 1)]

    steps = [both(first), both(along_u, -1), both(along_u, 1), both(along_v, 0, -1), both(along_v, 0, 1), both(along_u, 2)]
    for u in (-1, 1):
        steps += [both(along_v, u, -1), both(along_v, u, 1)]
    steps += [both(along_v, 0, 2), both(along_v, 2, -1), both(along_v, 2, 1)]
    steps += [both(along_v, u, 2) for u in (-1, 1, 2)]

    def finish():
        def one(k, carry):
            slab = 2 * k + 1 - core
            arrive(0, slab)
            arrive(1, slab)
            return carry

        lax.fori_loop(0, N_ENT // 2, one, 0)
        wait_bytes(table.at[pl.ds(0, N_ENT - 1)], send_sem)

    return steps + [finish]


def sweep(ref):
    size = ref.shape[0]
    rows = lax.broadcasted_iota(jnp.int32, (size, size), 0)
    lanes = lax.broadcasted_iota(jnp.int32, (size, size), 1)
    lane1 = lax.broadcasted_iota(jnp.int32, (1, size), 1)
    row1 = lax.broadcasted_iota(jnp.int32, (size, 1), 0)

    def pivot(k, carry):
        whole = ref[...]
        line = ref[pl.ds(k, 1), :]
        on_lane = lanes == k
        column = jnp.sum(jnp.where(on_lane, whole, 0.0), axis=1, keepdims=True)
        corner = jnp.sum(jnp.where(lane1 == k, line, 0.0), axis=1, keepdims=True)
        line = jnp.where(lane1 == k, -1.0, line) * (1.0 / corner)
        column = jnp.where(row1 == k, -1.0, column)
        ref[...] = jnp.where(on_lane | (rows == k), 0.0, whole) - column * line
        return carry

    return pivot


def sorted_sums(run, count, term, keep_at, start):
    def four(q, carry):
        for i in range(4):
            t = start + q * 4 + i
            run[t + 1] = run[t] * keep_at(t) + term(t)
        return carry

    lax.fori_loop(0, count // 4, four, 0)


def sweep_kernel(
    meta, keeps, needed, tiles, factors, cores, numer_out, inverse_out,
    table, run, terms, landed, req_out, req_in, gram_out, gram_in, gram_all, sys_out, sys_in, sys_all,
    core_wide, core_turn, corner, band, ring_send, ring_recv, pair_send, pair_recv,
):
    ent = lax.axis_index("ent")
    rel = lax.axis_index("rel")
    greet(ent, rel)

    def ask(o, carry):
        req_out[o] = jnp.full((8, 128), needed[o], jnp.int32)
        return carry

    lax.fori_loop(0, N_ENT, ask, 0)
    gram_out[...] = dot(factors[...], factors[...], ((0,), (0,))).reshape(N_ENT, 8, R)
    spread("ent", N_ENT, ent, lambda o: gram_out.at[o], gram_in, pair_send.at[0], pair_recv.at[0])
    gram_in[ent] = gram_out[ent]
    steps = ring_gather(ent, factors, table, ring_send.at[0], ring_recv)
    steps.pop(0)()
    spread("ent", N_ENT, ent, lambda o: req_out.at[o], req_in, pair_send.at[1], pair_recv.at[1])
    req_in[ent] = req_out[ent]
    table[ent] = factors[...]
    for j in range(REL_DEV):
        core_wide[j] = cores[j].astype(F32)
        core_turn[j] = core_wide[j].T
    run[0] = jnp.zeros((BLK, R), F32)

    def backward(t):
        own = factors[pl.ds(meta[4, t] * BLK, BLK), :]
        right = dot(tiles[meta[3, t]], own, ((0,), (0,))).astype(BF16)
        return dot(right, cores[meta[5, t]])

    def backward_part(q):
        sorted_sums(run, 16, backward, lambda t: keeps[1, t], q * 16)

    backward_part(0)
    spread_wait(N_ENT, gram_in, gram_out, pair_send.at[0], pair_recv.at[0])
    gram_all[ent] = jnp.sum(gram_in[...], axis=0)
    spread("ent", N_ENT, ent, lambda o: gram_all.at[ent], gram_all, pair_send.at[2], pair_recv.at[2])
    steps.pop(0)()
    backward_part(1)
    spread_wait(N_ENT, gram_all, gram_all, pair_send.at[2], pair_recv.at[2])
    gram = gram_all[...].reshape(R, R)
    mine = pl.ds(pl.multiple_of(ent * 8, 8), 8)
    part = jnp.zeros((8, R), F32)
    for j in range(REL_DEV):
        left = dot(core_wide[j, mine, :], gram, precision=HIGH)
        part = part + dot(left, core_turn[j], precision=HIGH)
        left = dot(core_turn[j, mine, :], gram, precision=HIGH)
        part = part + dot(left, core_wide[j], precision=HIGH)
    sys_out[...] = part
    spread("rel", N_REL, rel, lambda o: sys_out, sys_in, pair_send.at[3], pair_recv.at[3])
    sys_in[rel] = part
    steps.pop(0)()
    backward_part(2)
    spread_wait(N_REL, sys_in, sys_out, pair_send.at[3], pair_recv.at[3])
    unit = lax.broadcasted_iota(jnp.int32, (8, R), 0) + ent * 8 == lax.broadcasted_iota(jnp.int32, (8, R), 1)
    sys_all[ent] = jnp.sum(sys_in[...], axis=0) + jnp.where(unit, ridge_shift, 0.0)
    spread("ent", N_ENT, ent, lambda o: sys_all.at[ent], sys_all, pair_send.at[4], pair_recv.at[4])
    steps.pop(0)()
    backward_part(3)

    def pack(s, carry):
        terms[s] = (run[meta[7, s]] * keeps[3, s]).astype(BF16)
        return carry

    lax.fori_loop(0, N_ENT, pack, 0)
    spread("ent", N_ENT, ent, lambda o: terms.at[o], landed, pair_send.at[5], pair_recv.at[5])
    landed[ent] = terms[ent]
    spread_wait(N_ENT, sys_all, sys_all, pair_send.at[4], pair_recv.at[4])

    system = sys_all[...].reshape(R, R)
    corner[...] = system[:128, :128]
    band[...] = system[:128, 128:]
    pivot = sweep(corner)
    for i in range(4):
        steps.pop(0)()
        lax.fori_loop(i * 32, i * 32 + 32, pivot, 0)
    first = -corner[...]
    ahead = dot(first, band[...], precision=HIGH)
    low = sys_all[pl.ds(16, 16)].reshape(128, R)[:, 128:]
    corner[...] = low - dot(band[...], ahead, ((0,), (0,)), HIGH)
    for i in range(4):
        steps.pop(0)()
        lax.fori_loop(i * 32, i * 32 + 32, pivot, 0)
    second = -corner[...]
    mixed = dot(ahead, second, precision=HIGH)
    inverse_out[pl.ds(0, 128), pl.ds(0, 128)] = first + dot(mixed, ahead, ((1,), (1,)), HIGH)
    inverse_out[pl.ds(0, 128), pl.ds(128, 128)] = -mixed
    inverse_out[pl.ds(128, 128), pl.ds(0, 128)] = -mixed.T
    inverse_out[pl.ds(128, 128), pl.ds(128, 128)] = second

    for step in steps:
        step()

    def forward(t):
        return dot(tiles[meta[0, t]], table[meta[1, t], pl.ds(meta[2, t] * BLK, BLK), :])

    sorted_sums(run, TILES, forward, lambda t: keeps[0, t], 0)
    spread_wait(N_ENT, req_in, req_out, pair_send.at[1], pair_recv.at[1])
    spread_wait(N_ENT, landed, terms, pair_send.at[5], pair_recv.at[5])
    for b in range(ROWS):
        total = jnp.zeros((BLK, R), F32)
        for j in range(REL_DEV):
            g = j * ROWS + b
            summed = (run[meta[6, g]] * keeps[2, g]).astype(BF16)
            total = total + dot(summed, cores[j], ((1,), (1,)))
        run[b] = total

    def land(c, carry):
        chunk = pl.ds(pl.multiple_of(c * 32, 32), 32)

        def add(o, totals):
            data = landed[o, chunk, :].astype(F32)
            asked = jnp.tile(req_in[o], (4, 2))
            return tuple(totals[b] + jnp.where(asked == b, data, 0.0) for b in range(ROWS))

        totals = lax.fori_loop(0, N_ENT, add, tuple(run[b, chunk, :] for b in range(ROWS)))
        for b in range(ROWS):
            numer_out[pl.ds(pl.multiple_of(b * BLK + c * 32, 32), 32), :] = totals[b].astype(BF16)
        return carry

    lax.fori_loop(0, BLK // 32, land, 0)


def core_kernel(
    meta, keeps, tiles, numer, inverse, basis, spectrum, factors_out, cores_out,
    table, run, numer_in, slab, slice_out, sum_out, sum_in, sum_all, turned, weight,
    ring_send, ring_recv, pair_send, pair_recv,
):
    ent = lax.axis_index("ent")
    rel = lax.axis_index("rel")
    greet(ent, rel)
    piece = SLAB // N_REL

    def rows_of(ref, z):
        return ref.at[pl.ds(pl.multiple_of(z * piece, piece), piece)]

    spread("rel", N_REL, rel, lambda o: rows_of(numer, o), numer_in, pair_send.at[0], pair_recv.at[0])
    numer_in[rel] = numer[pl.ds(pl.multiple_of(rel * piece, piece), piece), :]
    wide = jnp.broadcast_to(spectrum[...], (R, R))
    weight[...] = 1.0 / (wide * wide.T + ridge_shift)
    turned[...] = basis[...].T
    run[0] = jnp.zeros((BLK, R), F32)
    spread_wait(N_REL, numer_in, numer, pair_send.at[0], pair_recv.at[0])
    total = jnp.sum(numer_in[...].astype(F32), axis=0)
    slab[rel] = dot(total, inverse[...], precision=HIGH).astype(BF16)
    spread("rel", N_REL, rel, lambda o: slab.at[rel], slab, pair_send.at[1], pair_recv.at[1])
    spread_wait(N_REL, slab, slab, pair_send.at[1], pair_recv.at[1])
    factors_out[...] = slab[...].reshape(SLAB, R)
    table[ent] = factors_out[...]
    for step in ring_gather(ent, factors_out, table, ring_send.at[0], ring_recv):
        step()

    def latest(t):
        return dot(tiles[meta[0, t]], table[meta[1, t], pl.ds(meta[2, t] * BLK, BLK), :])

    sorted_sums(run, TILES, latest, lambda t: keeps[0, t], 0)
    for j in range(REL_DEV):
        total = jnp.zeros((R, R), F32)
        for b in range(ROWS):
            g = j * ROWS + b
            summed = (run[meta[6, g]] * keeps[2, g]).astype(BF16)
            total = total + dot(factors_out[pl.ds(b * BLK, BLK), :], summed, ((0,), (0,)))
        sum_out[pl.ds(j * 16, 16)] = total.reshape(16, 16, R)
    spread("ent", N_ENT, ent, lambda o: sum_out.at[o], sum_in, pair_send.at[2], pair_recv.at[2])
    sum_in[ent] = sum_out[ent]
    spread_wait(N_ENT, sum_in, sum_out, pair_send.at[2], pair_recv.at[2])
    sum_all[ent] = jnp.sum(sum_in[...], axis=0)
    spread("ent", N_ENT, ent, lambda o: sum_all.at[ent], sum_all, pair_send.at[3], pair_recv.at[3])
    spread_wait(N_ENT, sum_all, sum_all, pair_send.at[3], pair_recv.at[3])
    for j in range(REL_DEV):
        projected = sum_all[pl.ds(j * 16, 16)].reshape(R, R)
        rotated = dot(turned[...], dot(projected, basis[...], precision=HIGH), precision=HIGH)
        rotated = rotated * weight[...]
        cores_out[j] = dot(basis[...], dot(rotated, turned[...], precision=HIGH), precision=HIGH)


def shards(tile_vals, tile_row, tile_rel, tile_src, needed, factors, cores, basis, spectrum):
    rows, rels, sources = tile_row[0, 0], tile_rel[0, 0], tile_src[0, 0]
    asked = needed[0, 0, :, 0]
    order = jnp.arange(TILES, dtype=jnp.int32)
    wanted = jnp.sum(jnp.where(sources[:, None] == jnp.arange(N_ENT)[None, :], asked[None, :], 0), axis=1)

    def arranged(keys, values, groups):
        before = (keys[None, :] < keys[:, None]) | ((keys[None, :] == keys[:, None]) & (order[None, :] < order[:, None]))
        rank = jnp.sum(before.astype(jnp.int32), axis=1)
        here = rank[None, :] == order[:, None]
        keys_sorted, *out = [jnp.sum(jnp.where(here, v[None, :], 0), axis=1) for v in (keys, *values)]
        keep = jnp.concatenate([jnp.zeros((1,), F32), (keys_sorted[1:] == keys_sorted[:-1]).astype(F32)])
        ids = jnp.arange(TILES, dtype=jnp.int32)
        upto = jnp.sum((keys[None, :] <= ids[:, None]).astype(jnp.int32), axis=1)
        some = jnp.any(keys[None, :] == ids[:, None], axis=1).astype(F32)
        return out, keep, upto, some

    fwd, fwd_keep, fwd_last, fwd_some = arranged(rels * ROWS + rows, (order, sources, wanted), 8)
    bwd, bwd_keep, bwd_last, bwd_some = arranged(sources, (order, rows, rels), 32)
    meta = jnp.stack([*fwd, *bwd, fwd_last, bwd_last])
    keeps = jnp.stack([fwd_keep, bwd_keep, fwd_some, bwd_some])
    smem, vmem = pl.BlockSpec(memory_space=pltpu.SMEM), pl.BlockSpec(memory_space=pltpu.VMEM)
    tiles = tile_vals[0, 0]
    ring = [pltpu.SemaphoreType.DMA((1,)), pltpu.SemaphoreType.DMA((2, N_ENT))]
    pairs = [pltpu.SemaphoreType.DMA((6,)), pltpu.SemaphoreType.DMA((6,))]

    numer, inverse = pl.pallas_call(
        sweep_kernel,
        out_shape=[jax.ShapeDtypeStruct((SLAB, R), BF16), jax.ShapeDtypeStruct((R, R), F32)],
        in_specs=[smem] * 3 + [vmem] * 3,
        out_specs=[vmem, vmem],
        scratch_shapes=[
            pltpu.VMEM((N_ENT, SLAB, R), BF16),
            pltpu.VMEM((TILES + 1, BLK, R), F32),
            pltpu.VMEM((N_ENT, BLK, R), BF16),
            pltpu.VMEM((N_ENT, BLK, R), BF16),
            pltpu.VMEM((N_ENT, 8, 128), jnp.int32),
            pltpu.VMEM((N_ENT, 8, 128), jnp.int32),
            pltpu.VMEM((N_ENT, 8, R), F32),
            pltpu.VMEM((N_ENT, 8, R), F32),
            pltpu.VMEM((N_ENT, 8, R), F32),
            pltpu.VMEM((8, R), F32),
            pltpu.VMEM((N_REL, 8, R), F32),
            pltpu.VMEM((N_ENT, 8, R), F32),
            pltpu.VMEM((REL_DEV, R, R), F32),
            pltpu.VMEM((REL_DEV, R, R), F32),
            pltpu.VMEM((128, 128), F32),
            pltpu.VMEM((128, 128), F32),
            *ring,
            *pairs,
        ],
        compiler_params=pltpu.CompilerParams(collective_id=0, has_side_effects=True, vmem_limit_bytes=48 << 20),
        name="numerator_and_inverse",
    )(meta, keeps, asked, tiles, factors, cores)
    return pl.pallas_call(
        core_kernel,
        out_shape=[jax.ShapeDtypeStruct((SLAB, R), BF16), jax.ShapeDtypeStruct((REL_DEV, R, R), F32)],
        in_specs=[smem] * 2 + [vmem] * 5,
        out_specs=[vmem, vmem],
        scratch_shapes=[
            pltpu.VMEM((N_ENT, SLAB, R), BF16),
            pltpu.VMEM((TILES + 1, BLK, R), F32),
            pltpu.VMEM((N_REL, SLAB // N_REL, R), BF16),
            pltpu.VMEM((N_REL, SLAB // N_REL, R), BF16),
            pltpu.VMEM((SLAB // N_REL, R), BF16),
            pltpu.VMEM((N_ENT, 16, R), F32),
            pltpu.VMEM((N_ENT, 16, R), F32),
            pltpu.VMEM((N_ENT, 16, R), F32),
            pltpu.VMEM((R, R), F32),
            pltpu.VMEM((R, R), F32),
            *ring,
            *pairs,
        ],
        compiler_params=pltpu.CompilerParams(collective_id=1, has_side_effects=True, vmem_limit_bytes=48 << 20),
        name="factors_and_cores",
    )(meta, keeps, tiles, numer, inverse, basis, spectrum.reshape(1, R))


def solution(mesh):
    in_specs = (
        P("ent", "rel", None, None, None),
        P("ent", "rel", None),
        P("ent", "rel", None),
        P("ent", "rel", None),
        P("ent", "rel", None, None),
        P("ent", None),
        P("rel", None, None),
        P(),
        P(),
    )
    out_specs = (P("ent", None), P("rel", None, None))
    return jax.shard_map(
        lambda *args: tuple(shards(*args)), mesh=mesh, in_specs=in_specs, out_specs=out_specs, check_vma=False
    )
```

```python
import functools
import jax
import jax.numpy as jnp
from jax import lax
from jax.experimental import pallas as pl
from jax.experimental.pallas import tpu as pltpu
from jax.sharding import PartitionSpec as P

ridge_shift = 1.0
N_ENT, N_REL = 32, 8
BLK, R, ROWS, TILES, REL_DEV, SLAB = 128, 256, 4, 64, 2, 512
PIECE = SLAB // N_REL
MESH = pl.DeviceIdType.MESH
F32, BF16 = jnp.float32, jnp.bfloat16
HIGH = lax.Precision.HIGHEST
SPOT = {0: 0, -1: 1, 1: 2, 2: 3}


def dot(a, b, dims=((1,), (0,)), precision=None):
    return lax.dot_general(a, b, (dims, ((), ())), precision=precision, preferred_element_type=F32)


def send(src, dst, send_sem, recv_sem, target):
    return pltpu.make_async_remote_copy(
        src_ref=src, dst_ref=dst, send_sem=send_sem, recv_sem=recv_sem, device_id=target, device_id_type=MESH
    )


def wait_bytes(ref, sem):
    pltpu.make_async_copy(ref, ref, sem).wait()


def greet(me_ent, me_rel):
    barrier = pltpu.get_barrier_semaphore()

    def ent_signal(k, carry):
        pl.semaphore_signal(barrier, inc=1, device_id={"ent": lax.rem(me_ent + k, N_ENT)}, device_id_type=MESH)
        return carry

    def rel_signal(k, carry):
        pl.semaphore_signal(barrier, inc=1, device_id={"rel": lax.rem(me_rel + k, N_REL)}, device_id_type=MESH)
        return carry

    lax.fori_loop(1, N_ENT, ent_signal, 0)
    lax.fori_loop(1, N_REL, rel_signal, 0)
    return lambda: pl.semaphore_wait(barrier, N_ENT + N_REL - 2)


def pieces(wide, count):
    out = []
    for _ in range(count):
        out.append(wide.astype(BF16))
        wide = wide - out[-1].astype(F32)
    return out


def dot_pieces(left, right, dims=((1,), (0,))):
    longest = max(len(left), len(right))
    terms = [(i + k, dot(a, b, dims)) for i, a in enumerate(left) for k, b in enumerate(right) if i + k < longest]
    return sum(t for _, t in sorted(terms, key=lambda p: -p[0]))


def spread(axis, count, me, source_at, landing, send_sem, recv_sem):
    def one(k, carry):
        other = lax.rem(me + k, count)
        send(source_at(other), landing.at[me], send_sem, recv_sem, {axis: other}).start()
        return carry

    lax.fori_loop(1, count, one, 0)


def spread_wait(count, landing, source, send_sem, recv_sem):
    wait_bytes(landing.at[pl.ds(0, count - 1)], recv_sem)
    wait_bytes(landing.at[pl.ds(0, count - 1)], send_sem)


def ring_gather(me, own, table, send_sem, recv_sem):
    core = lax.rem(me, 2)
    col = lax.rem(me // 2, 4)
    row = me // 8
    way = 1 - 2 * core
    sibling = me + way

    def at(h, u, v):
        du, dv = (u, v) if h == 0 else (v, u)
        x = lax.rem(col + du * way + 8, 4)
        y = lax.rem(row + dv * way + 8, 4)
        return (y * 4 + x) * 2 + core

    def part(ref, h):
        return ref.at[pl.ds(h * N_REL // 2, N_REL // 2)]

    def go(h, u, v, target):
        slab = at(h, u, v)
        dst = part(table.at[slab], h)
        src = part(own, h) if (u, v) == (0, 0) else dst
        send(src, dst, send_sem, recv_sem.at[h, slab], {"ent": target}).start()

    def arrive(h, slab):
        dst = part(table.at[slab], h)
        pltpu.make_async_copy(dst, dst, recv_sem.at[h, slab]).wait()

    def first(h):
        go(h, 0, 0, at(h, 1, 0))
        go(h, 0, 0, at(h, -1, 0))
        go(h, 0, 0, at(h, 0, 1))
        go(h, 0, 0, at(h, 0, -1))
        go(h, 0, 0, sibling)

    def along_u(h, u):
        arrive(h, at(h, u, 0))
        if u == -1:
            go(h, u, 0, at(h, 1, 0))
        go(h, u, 0, at(h, 0, 1))
        go(h, u, 0, at(h, 0, -1))
        go(h, u, 0, sibling)

    def along_v(h, u, v):
        arrive(h, at(h, u, v))
        if v == -1:
            go(h, u, v, at(h, 0, 1))
        go(h, u, v, sibling)

    def both(act, *where):
        return lambda: [act(h, *where) for h in (0, 1)]

    steps = [both(first), both(along_u, -1), both(along_u, 1), both(along_v, 0, -1), both(along_v, 0, 1), both(along_u, 2)]
    for u in (-1, 1):
        steps += [both(along_v, u, -1), both(along_v, u, 1)]
    steps += [both(along_v, 0, 2), both(along_v, 2, -1), both(along_v, 2, 1)]
    steps += [both(along_v, u, 2) for u in (-1, 1, 2)]

    def finish():
        def one(k, carry):
            slab = 2 * k + 1 - core
            arrive(0, slab)
            arrive(1, slab)
            return carry

        lax.fori_loop(0, N_ENT // 2, one, 0)
        wait_bytes(table.at[pl.ds(0, N_ENT - 1)], send_sem)

    return steps + [finish]


def sweep(ref):
    size = ref.shape[0]
    rows = lax.broadcasted_iota(jnp.int32, (size, size), 0)
    lanes = lax.broadcasted_iota(jnp.int32, (size, size), 1)
    lane1 = lax.broadcasted_iota(jnp.int32, (1, size), 1)
    row1 = lax.broadcasted_iota(jnp.int32, (size, 1), 0)

    def pivot(k, carry):
        whole = ref[...]
        line = ref[pl.ds(k, 1), :]
        on_lane = lanes == k
        column = jnp.sum(jnp.where(on_lane, whole, 0.0), axis=1, keepdims=True)
        corner = jnp.sum(jnp.where(lane1 == k, line, 0.0), axis=1, keepdims=True)
        line = jnp.where(lane1 == k, -1.0, line) * (1.0 / corner)
        column = jnp.where(row1 == k, -1.0, column)
        ref[...] = jnp.where(on_lane | (rows == k), 0.0, whole) - column * line
        return carry

    return pivot


def sorted_sums(run, count, term, keep_at, start):
    def four(q, carry):
        for i in range(4):
            t = start + q * 4 + i
            run[t + 1] = run[t] * keep_at(t) + term(t)
        return carry

    lax.fori_loop(0, count // 4, four, 0)


def arranged(raw, key):
    shape = (128, 128)
    lane = lax.broadcasted_iota(jnp.int32, shape, 1)
    keys = jnp.broadcast_to(raw[key : key + 1, :], shape)
    turned = keys.T
    earlier = (keys == turned) & (lane < lax.broadcasted_iota(jnp.int32, shape, 0))
    rank = jnp.sum(jnp.where((keys < turned) | earlier, 1, 0), axis=1, keepdims=True)
    repeats = jnp.sum(jnp.where(earlier, 1, 0), axis=1, keepdims=True)
    here = rank == lane

    def put(values):
        return jnp.sum(jnp.where(here, values, 0), axis=0, keepdims=True)

    keep = put(jnp.where(repeats > 0, 1, 0))
    upto = jnp.sum(jnp.where(turned <= lane, 1, 0), axis=0, keepdims=True)
    some = jnp.minimum(jnp.sum(jnp.where(turned == lane, 1, 0), axis=0, keepdims=True), 1)
    return put, keep, upto, some


def sweep_kernel(
    rows_in, rels_in, sources_in, needed_in, needed, tiles_hbm, factors_hbm, cores_hbm, basis_hbm, spectrum,
    factors_out, cores_out,
    tiles, factors, cores, basis, raw, meta_wide, keeps_wide, meta, keeps,
    table, fresh, run, ahead_terms, terms, landed, req_out, req_in, sys_out, sys_in, sys_row, sys_rows, sys_all,
    corner, band, inverse, numer_out, numer_in, weight, sum_out, sum_in, sum_all,
    ring_send, ring_recv, pair_send, pair_recv, local,
):
    ent = lax.axis_index("ent")
    rel = lax.axis_index("rel")
    moves = [
        pltpu.make_async_copy(a, b, local.at[i])
        for i, (a, b) in enumerate(
            ((factors_hbm, factors), (cores_hbm, cores), (tiles_hbm, tiles), (basis_hbm, basis))
        )
    ]
    for move in moves:
        move.start()
    all_here = greet(ent, rel)

    moves[0].wait()
    moves[1].wait()
    slab_rows = factors[...].reshape(SLAB, R)
    gram = pieces(dot(slab_rows, slab_rows, ((0,), (0,))), 3)
    share = jnp.zeros((R, R), F32)
    for j in range(REL_DEV):
        left = pieces(dot_pieces([cores[j]], gram), 3)
        share = share + dot_pieces(left, [cores[j]], ((1,), (1,)))
        right = pieces(dot_pieces(gram, [cores[j]]), 3)
        share = share + dot_pieces([cores[j]], right, ((0,), (0,)))
    sys_out[...] = share.reshape(N_ENT, 8, R)
    all_here()
    spread("ent", N_ENT, ent, lambda o: sys_out.at[o], sys_in, pair_send.at[0], pair_recv.at[0])
    sys_in[ent] = sys_out[ent]
    steps = ring_gather(ent, factors, table, ring_send.at[0], ring_recv.at[0])
    steps.pop(0)()

    raw[...] = jnp.full((8, 128), 1000, jnp.int32)
    raw[0:1, 0:TILES] = rels_in[...] * ROWS + rows_in[...]
    raw[1:2, 0:TILES] = sources_in[...]
    raw[2:3, 0:TILES] = rows_in[...]
    raw[3:4, 0:TILES] = rels_in[...]
    raw[4:5, 0:N_ENT] = needed_in[...]
    lane = lax.broadcasted_iota(jnp.int32, (128, 128), 1)
    line = lax.broadcasted_iota(jnp.int32, (128, 128), 0)

    def turn(i):
        return jnp.broadcast_to(raw[i : i + 1, :], (128, 128)).T

    wanted = jnp.sum(jnp.where(lane == turn(1), jnp.broadcast_to(raw[4:5, :], (128, 128)), 0), axis=1, keepdims=True)
    put, keep, upto, some = arranged(raw, 0)
    meta_wide[0:1, :] = put(line)
    meta_wide[1:2, :] = put(turn(1))
    meta_wide[2:3, :] = put(wanted)
    meta_wide[6:7, :] = upto
    keeps_wide[0:1, :] = keep.astype(F32)
    keeps_wide[2:3, :] = some.astype(F32)
    put, keep, upto, some = arranged(raw, 1)
    meta_wide[3:4, :] = put(line)
    meta_wide[4:5, :] = put(turn(2))
    meta_wide[5:6, :] = put(turn(3))
    meta_wide[7:8, :] = upto
    keeps_wide[1:2, :] = keep.astype(F32)
    keeps_wide[3:4, :] = some.astype(F32)
    keeps_wide[4:8, :] = jnp.zeros((4, 128), F32)
    orders = [
        pltpu.make_async_copy(meta_wide, meta, local.at[4]),
        pltpu.make_async_copy(keeps_wide, keeps, local.at[5]),
    ]
    for order in orders:
        order.start()

    def ask(o, carry):
        req_out[o] = jnp.full((8, 128), needed[0, o], jnp.int32)
        return carry

    lax.fori_loop(0, N_ENT, ask, 0)
    req_in[ent] = req_out[ent]
    spread("ent", N_ENT, ent, lambda o: req_out.at[o], req_in, pair_send.at[1], pair_recv.at[1])
    table[ent] = factors[...]
    run[0] = jnp.zeros((BLK, R), F32)
    for order in orders:
        order.wait()
    moves[2].wait()

    def backward(t):
        own = factors[pl.ds(meta[4, t] * 2, 2)].reshape(BLK, R)
        right = dot(tiles[meta[3, t]], own, ((0,), (0,))).astype(BF16)
        return dot(right, cores[meta[5, t]])

    def backward_part(q):
        sorted_sums(run, 16, backward, lambda t: keeps[1, t], q * 16)

    backward_part(0)
    spread_wait(N_ENT, sys_in, sys_out, pair_send.at[0], pair_recv.at[0])
    sys_row[...] = jnp.sum(sys_in[...], axis=0)
    spread("rel", N_REL, rel, lambda o: sys_row, sys_rows, pair_send.at[3], pair_recv.at[3])
    sys_rows[rel] = sys_row[...]
    steps.pop(0)()
    backward_part(1)
    steps.pop(0)()
    backward_part(2)
    spread_wait(N_REL, sys_rows, sys_row, pair_send.at[3], pair_recv.at[3])
    unit = lax.broadcasted_iota(jnp.int32, (8, R), 0) + ent * 8 == lax.broadcasted_iota(jnp.int32, (8, R), 1)
    sys_all[ent] = jnp.sum(sys_rows[...], axis=0) + jnp.where(unit, ridge_shift, 0.0)
    spread("ent", N_ENT, ent, lambda o: sys_all.at[ent], sys_all, pair_send.at[4], pair_recv.at[4])
    steps.pop(0)()
    backward_part(3)
    steps.pop(0)()

    def pack(o):
        return (run[meta[7, o]] * keeps[3, o]).astype(BF16)

    def give(k, carry):
        o = lax.rem(ent + k, N_ENT)
        terms[o] = pack(o)
        send(terms.at[o], landed.at[ent], pair_send.at[5], pair_recv.at[5], {"ent": o}).start()
        return carry

    lax.fori_loop(1, N_ENT, give, 0)
    landed[ent] = pack(ent)
    steps.pop(0)()
    spread_wait(N_ENT, sys_all, sys_all, pair_send.at[4], pair_recv.at[4])

    system = sys_all[...].reshape(R, R)
    corner[...] = system[:128, :128]
    band[...] = system[:128, 128:]
    pivot = sweep(corner)

    def pivots():
        for i in range(8):
            if len(steps) > 1:
                steps.pop(0)()
            lax.fori_loop(i * 16, i * 16 + 16, pivot, 0)

    pivots()
    first = -corner[...]
    ahead = dot(first, band[...], precision=HIGH)
    low = sys_all[pl.ds(16, 16)].reshape(128, R)[:, 128:]
    corner[...] = low - dot(band[...], ahead, ((0,), (0,)), HIGH)
    inverse[pl.ds(0, 128), pl.ds(0, 128)] = first
    band[...] = ahead
    pivots()
    ahead = band[...]
    second = -corner[...]
    mixed = dot(ahead, second, precision=HIGH)
    inverse[pl.ds(0, 128), pl.ds(0, 128)] += dot(mixed, ahead, ((1,), (1,)), HIGH)
    inverse[pl.ds(0, 128), pl.ds(128, 128)] = -mixed
    inverse[pl.ds(128, 128), pl.ds(0, 128)] = -mixed.T
    inverse[pl.ds(128, 128), pl.ds(128, 128)] = second

    for step in steps:
        step()

    def forward(t):
        return dot(tiles[meta[0, t]], table[meta[1, t], pl.ds(meta[2, t] * 2, 2)].reshape(BLK, R))

    sorted_sums(run, TILES, forward, lambda t: keeps[0, t], 0)
    for b in range(ROWS):
        total = jnp.zeros((BLK, R), F32)
        for j in range(REL_DEV):
            g = j * ROWS + b
            summed = (run[meta[6, g]] * keeps[2, g]).astype(BF16)
            total = total + dot(summed, cores[j], ((1,), (1,)))
        ahead_terms[pl.ds(b * 2, 2)] = total.reshape(2, PIECE, R)
    moves[3].wait()
    wide = jnp.broadcast_to(spectrum[...], (R, R))
    weight[...] = 1.0 / (wide * wide.T + ridge_shift)
    spread_wait(N_ENT, req_in, req_out, pair_send.at[1], pair_recv.at[1])
    spread_wait(N_ENT, landed, terms, pair_send.at[5], pair_recv.at[5])

    def landing(q):
        block = q // 2
        chunk = pl.ds(pl.multiple_of(lax.rem(q, 2) * PIECE, PIECE), PIECE)

        def add(o, total):
            return total + jnp.where(jnp.tile(req_in[o], (8, 2)) == block, landed[o, chunk, :].astype(F32), 0.0)

        return lax.fori_loop(0, N_ENT, add, ahead_terms[q])

    def hand_over(k, carry):
        z = lax.rem(rel + k, N_REL)
        numer_out[z] = landing(z).astype(BF16)
        send(numer_out.at[z], numer_in.at[rel], pair_send.at[2], pair_recv.at[2], {"rel": z}).start()
        return carry

    lax.fori_loop(1, N_REL, hand_over, 0)
    numer_in[rel] = jnp.zeros((PIECE, R), BF16)
    mine = landing(rel)
    spread_wait(N_REL, numer_in, numer_out, pair_send.at[2], pair_recv.at[2])
    total = mine + jnp.sum(numer_in[...].astype(F32), axis=0)
    fresh[ent, rel] = dot(total, inverse[...], precision=HIGH).astype(BF16)
    spread("rel", N_REL, rel, lambda o: fresh.at[ent, rel], fresh.at[ent], pair_send.at[6], pair_recv.at[6])
    basis_wide = pieces(basis[...], 2)
    turned = pieces(basis[...].T, 2)
    spread_wait(N_REL, fresh.at[ent], fresh.at[ent], pair_send.at[6], pair_recv.at[6])
    steps = ring_gather(ent, fresh.at[ent], fresh, ring_send.at[1], ring_recv.at[1])
    steps.pop(0)()
    factors_out[...] = fresh[ent].reshape(SLAB, R)
    for step in steps:
        step()

    def latest(t):
        return dot(tiles[meta[0, t]], fresh[meta[1, t], pl.ds(meta[2, t] * 2, 2)].reshape(BLK, R))

    sorted_sums(run, TILES, latest, lambda t: keeps[0, t], 0)
    for j in range(REL_DEV):
        total = jnp.zeros((R, R), F32)
        for b in range(ROWS):
            g = j * ROWS + b
            summed = (run[meta[6, g]] * keeps[2, g]).astype(BF16)
            total = total + dot(fresh[ent, pl.ds(b * 2, 2)].reshape(BLK, R), summed, ((0,), (0,)))
        sum_out[pl.ds(j * 16, 16)] = total.astype(BF16).reshape(16, 16, R)
    spread("ent", N_ENT, ent, lambda o: sum_out.at[o], sum_in, pair_send.at[7], pair_recv.at[7])
    sum_in[ent] = sum_out[ent]
    spread_wait(N_ENT, sum_in, sum_out, pair_send.at[7], pair_recv.at[7])
    sum_all[ent] = jnp.sum(sum_in[...].astype(F32), axis=0).astype(BF16)
    spread("ent", N_ENT, ent, lambda o: sum_all.at[ent], sum_all, pair_send.at[8], pair_recv.at[8])
    spread_wait(N_ENT, sum_all, sum_all, pair_send.at[8], pair_recv.at[8])
    for j in range(REL_DEV):
        projected = sum_all[pl.ds(j * 16, 16)].reshape(R, R)
        half = pieces(dot_pieces([projected], basis_wide), 2)
        rotated = pieces(dot_pieces(turned, half) * weight[...], 2)
        half = pieces(dot_pieces(rotated, turned), 2)
        cores_out[j] = dot_pieces(basis_wide, half)


def shards(tile_vals, tile_row, tile_rel, tile_src, needed, factors, cores, basis, spectrum):
    smem, vmem = pl.BlockSpec(memory_space=pltpu.SMEM), pl.BlockSpec(memory_space=pltpu.VMEM)
    hbm = pl.BlockSpec(memory_space=pl.ANY)
    asked = needed.reshape(1, N_ENT)
    return pl.pallas_call(
        sweep_kernel,
        out_shape=[jax.ShapeDtypeStruct((SLAB, R), BF16), jax.ShapeDtypeStruct((REL_DEV, R, R), F32)],
        in_specs=[vmem] * 4 + [smem] + [hbm] * 4 + [vmem],
        out_specs=[vmem, vmem],
        scratch_shapes=[
            pltpu.VMEM((TILES, BLK, BLK), BF16),
            pltpu.VMEM((N_REL, PIECE, R), BF16),
            pltpu.VMEM((REL_DEV, R, R), BF16),
            pltpu.VMEM((R, R), F32),
            pltpu.VMEM((8, 128), jnp.int32),
            pltpu.VMEM((8, 128), jnp.int32),
            pltpu.VMEM((8, 128), F32),
            pltpu.SMEM((8, 128), jnp.int32),
            pltpu.SMEM((8, 128), F32),
            pltpu.VMEM((N_ENT, N_REL, PIECE, R), BF16),
            pltpu.VMEM((N_ENT, N_REL, PIECE, R), BF16),
            pltpu.VMEM((TILES + 1, BLK, R), F32),
            pltpu.VMEM((N_REL, PIECE, R), F32),
            pltpu.VMEM((N_ENT, BLK, R), BF16),
            pltpu.VMEM((N_ENT, BLK, R), BF16),
            pltpu.VMEM((N_ENT, 8, 128), jnp.int32),
            pltpu.VMEM((N_ENT, 8, 128), jnp.int32),
            pltpu.VMEM((N_ENT, 8, R), F32),
            pltpu.VMEM((N_ENT, 8, R), F32),
            pltpu.VMEM((8, R), F32),
            pltpu.VMEM((N_REL, 8, R), F32),
            pltpu.VMEM((N_ENT, 8, R), F32),
            pltpu.VMEM((128, 128), F32),
            pltpu.VMEM((128, 128), F32),
            pltpu.VMEM((R, R), F32),
            pltpu.VMEM((N_REL, PIECE, R), BF16),
            pltpu.VMEM((N_REL, PIECE, R), BF16),
            pltpu.VMEM((R, R), F32),
            pltpu.VMEM((N_ENT, 16, R), BF16),
            pltpu.VMEM((N_ENT, 16, R), BF16),
            pltpu.VMEM((N_ENT, 16, R), BF16),
            pltpu.SemaphoreType.DMA((2,)),
            pltpu.SemaphoreType.DMA((2, 2, N_ENT)),
            pltpu.SemaphoreType.DMA((9,)),
            pltpu.SemaphoreType.DMA((9,)),
            pltpu.SemaphoreType.DMA((6,)),
        ],
        compiler_params=pltpu.CompilerParams(collective_id=0, has_side_effects=True, vmem_limit_bytes=58 << 20),
        name="sweep",
    )(
        tile_row[0],
        tile_rel[0],
        tile_src[0],
        asked,
        asked,
        tile_vals[0, 0],
        factors.reshape(N_REL, PIECE, R),
        cores,
        basis,
        spectrum.reshape(1, R),
    )


def solution(mesh):
    in_specs = (
        P("ent", "rel", None, None, None),
        P("ent", "rel", None),
        P("ent", "rel", None),
        P("ent", "rel", None),
        P("ent", "rel", None, None),
        P("ent", None),
        P("rel", None, None),
        P(),
        P(),
    )
    out_specs = (P("ent", None), P("rel", None, None))
    return jax.shard_map(
        lambda *args: tuple(shards(*args)), mesh=mesh, in_specs=in_specs, out_specs=out_specs, check_vma=False
    )
```

```python
import functools
import jax
import jax.numpy as jnp
from jax import lax
from jax.experimental import pallas as pl
from jax.experimental.pallas import tpu as pltpu
from jax.sharding import PartitionSpec as P

ridge_shift = 1.0
N_ENT, N_REL = 32, 8
BLK, R, ROWS, TILES, REL_DEV, SLAB = 128, 256, 4, 64, 2, 512
PIECE = SLAB // N_REL
MESH = pl.DeviceIdType.MESH
F32, BF16 = jnp.float32, jnp.bfloat16
HIGH = lax.Precision.HIGHEST
SPOT = {0: 0, -1: 1, 1: 2, 2: 3}


def dot(a, b, dims=((1,), (0,)), precision=None):
    return lax.dot_general(a, b, (dims, ((), ())), precision=precision, preferred_element_type=F32)


def send(src, dst, send_sem, recv_sem, target):
    return pltpu.make_async_remote_copy(
        src_ref=src, dst_ref=dst, send_sem=send_sem, recv_sem=recv_sem, device_id=target, device_id_type=MESH
    )


def wait_bytes(ref, sem):
    pltpu.make_async_copy(ref, ref, sem).wait()


def greet(me_ent, me_rel):
    barrier = pltpu.get_barrier_semaphore()

    def ent_signal(k, carry):
        pl.semaphore_signal(barrier, inc=1, device_id={"ent": lax.rem(me_ent + k, N_ENT)}, device_id_type=MESH)
        return carry

    def rel_signal(k, carry):
        pl.semaphore_signal(barrier, inc=1, device_id={"rel": lax.rem(me_rel + k, N_REL)}, device_id_type=MESH)
        return carry

    lax.fori_loop(1, N_ENT, ent_signal, 0)
    lax.fori_loop(1, N_REL, rel_signal, 0)
    return lambda: pl.semaphore_wait(barrier, N_ENT + N_REL - 2)


def pieces(wide, count):
    out = []
    for _ in range(count):
        out.append(wide.astype(BF16))
        wide = wide - out[-1].astype(F32)
    return out


def dot_pieces(left, right, dims=((1,), (0,))):
    longest = max(len(left), len(right))
    terms = [(i + k, dot(a, b, dims)) for i, a in enumerate(left) for k, b in enumerate(right) if i + k < longest]
    return sum(t for _, t in sorted(terms, key=lambda p: -p[0]))


def spread(axis, count, me, source_at, landing, send_sem, recv_sem):
    def one(k, carry):
        other = lax.rem(me + k, count)
        send(source_at(other), landing.at[me], send_sem, recv_sem, {axis: other}).start()
        return carry

    lax.fori_loop(1, count, one, 0)


def spread_wait(count, landing, source, send_sem, recv_sem):
    wait_bytes(landing.at[pl.ds(0, count - 1)], recv_sem)
    wait_bytes(landing.at[pl.ds(0, count - 1)], send_sem)


def ring_gather(me, own, table, send_sem, recv_sem):
    core = lax.rem(me, 2)
    col = lax.rem(me // 2, 4)
    row = me // 8
    way = 1 - 2 * core
    sibling = me + way

    def at(h, u, v):
        du, dv = (u, v) if h == 0 else (v, u)
        x = lax.rem(col + du * way + 8, 4)
        y = lax.rem(row + dv * way + 8, 4)
        return (y * 4 + x) * 2 + core

    def part(ref, h):
        return ref.at[pl.ds(h * N_REL // 2, N_REL // 2)]

    def go(h, u, v, target):
        slab = at(h, u, v)
        dst = part(table.at[slab], h)
        src = part(own, h) if (u, v) == (0, 0) else dst
        send(src, dst, send_sem, recv_sem.at[h, slab], {"ent": target}).start()

    def arrive(h, slab):
        dst = part(table.at[slab], h)
        pltpu.make_async_copy(dst, dst, recv_sem.at[h, slab]).wait()

    def first(h):
        go(h, 0, 0, at(h, 1, 0))
        go(h, 0, 0, at(h, -1, 0))
        go(h, 0, 0, at(h, 0, 1))
        go(h, 0, 0, at(h, 0, -1))
        go(h, 0, 0, sibling)

    def along_u(h, u):
        arrive(h, at(h, u, 0))
        if u == -1:
            go(h, u, 0, at(h, 1, 0))
        go(h, u, 0, at(h, 0, 1))
        go(h, u, 0, at(h, 0, -1))
        go(h, u, 0, sibling)

    def along_v(h, u, v):
        arrive(h, at(h, u, v))
        if v == -1:
            go(h, u, v, at(h, 0, 1))
        go(h, u, v, sibling)

    def both(act, *where):
        return lambda: [act(h, *where) for h in (0, 1)]

    steps = [both(first), both(along_u, -1), both(along_u, 1), both(along_v, 0, -1), both(along_v, 0, 1), both(along_u, 2)]
    for u in (-1, 1):
        steps += [both(along_v, u, -1), both(along_v, u, 1)]
    steps += [both(along_v, 0, 2), both(along_v, 2, -1), both(along_v, 2, 1)]
    steps += [both(along_v, u, 2) for u in (-1, 1, 2)]

    def finish():
        def one(k, carry):
            slab = 2 * k + 1 - core
            arrive(0, slab)
            arrive(1, slab)
            return carry

        lax.fori_loop(0, N_ENT // 2, one, 0)
        wait_bytes(table.at[pl.ds(0, N_ENT - 1)], send_sem)

    return steps + [finish]


def sweep(ref, spread_column):
    size = ref.shape[0]
    rows = lax.broadcasted_iota(jnp.int32, (size, size), 0)
    lanes = lax.broadcasted_iota(jnp.int32, (size, size), 1)
    lane1 = lax.broadcasted_iota(jnp.int32, (1, size), 1)

    def column_of(whole, k):
        return jnp.broadcast_to(jnp.sum(jnp.where(lanes == k, whole, 0.0), axis=1, keepdims=True), (size, size))

    def pivot(k, column, line):
        whole = ref[...]
        later = jnp.minimum(k + 1, size - 1)
        next_column = column_of(whole, k + 1)
        next_line = ref[pl.ds(later, 1), :]
        spread_column[...] = column
        scale = 1.0 / spread_column[pl.ds(k, 1), :]
        factor = spread_column[pl.ds(later, 1), :]
        line = jnp.where(lane1 == k, -1.0, line) * scale
        column = jnp.where(rows == k, -1.0, column)
        ref[...] = jnp.where((lanes == k) | (rows == k), 0.0, whole) - column * line
        next_column = jnp.where(rows == k, 0.0, next_column) - column * (factor * scale)
        next_line = jnp.where(lane1 == k, 0.0, next_line) - factor * line
        return next_column, next_line

    def start():
        return column_of(ref[...], 0), ref[0:1, :]

    def some(k, count, carry):
        def four(q, carry):
            for i in range(4):
                carry = pivot(k + q * 4 + i, *carry)
            return carry

        return lax.fori_loop(0, count // 4, four, carry)

    return start, some


def sorted_sums(run, count, term, keep_at, start):
    def four(q, carry):
        for i in range(4):
            t = start + q * 4 + i
            run[t + 1] = run[t] * keep_at(t) + term(t)
        return carry

    lax.fori_loop(0, count // 4, four, 0)


def arranged(raw, key):
    shape = (128, 128)
    lane = lax.broadcasted_iota(jnp.int32, shape, 1)
    keys = jnp.broadcast_to(raw[key : key + 1, :], shape)
    turned = keys.T
    earlier = (keys == turned) & (lane < lax.broadcasted_iota(jnp.int32, shape, 0))
    rank = jnp.sum(jnp.where((keys < turned) | earlier, 1, 0), axis=1, keepdims=True)
    repeats = jnp.sum(jnp.where(earlier, 1, 0), axis=1, keepdims=True)
    here = rank == lane

    def put(values):
        return jnp.sum(jnp.where(here, values, 0), axis=0, keepdims=True)

    keep = put(jnp.where(repeats > 0, 1, 0))
    upto = jnp.sum(jnp.where(turned <= lane, 1, 0), axis=0, keepdims=True)
    some = jnp.minimum(jnp.sum(jnp.where(turned == lane, 1, 0), axis=0, keepdims=True), 1)
    return put, keep, upto, some


def sweep_kernel(
    rows_in, rels_in, sources_in, needed_in, needed, tiles_hbm, factors_hbm, cores_hbm, basis_hbm, spectrum,
    factors_out, cores_out,
    tiles, factors, cores, basis, raw, meta_wide, keeps_wide, meta, keeps,
    table, fresh, run, ahead_terms, terms, landed, req_out, req_in, sys_out, sys_in, sys_row, sys_rows, sys_all,
    corner, spread_column, band, inverse, numer_out, numer_in, weight, sum_out, sum_in, sum_all,
    ring_send, ring_recv, pair_send, pair_recv, local,
):
    ent = lax.axis_index("ent")
    rel = lax.axis_index("rel")
    moves = [
        pltpu.make_async_copy(a, b, local.at[i])
        for i, (a, b) in enumerate(
            ((factors_hbm, factors), (cores_hbm, cores), (tiles_hbm, tiles), (basis_hbm, basis))
        )
    ]
    for move in moves:
        move.start()
    all_here = greet(ent, rel)

    moves[0].wait()
    moves[1].wait()
    slab_rows = factors[...].reshape(SLAB, R)
    gram = pieces(dot(slab_rows, slab_rows, ((0,), (0,))), 3)
    share = jnp.zeros((R, R), F32)
    for j in range(REL_DEV):
        left = pieces(dot_pieces([cores[j]], gram), 3)
        share = share + dot_pieces(left, [cores[j]], ((1,), (1,)))
        right = pieces(dot_pieces(gram, [cores[j]]), 3)
        share = share + dot_pieces([cores[j]], right, ((0,), (0,)))
    sys_out[...] = share.reshape(N_ENT, 8, R)
    all_here()
    spread("ent", N_ENT, ent, lambda o: sys_out.at[o], sys_in, pair_send.at[0], pair_recv.at[0])
    sys_in[ent] = sys_out[ent]
    steps = ring_gather(ent, factors, table, ring_send.at[0], ring_recv.at[0])
    steps.pop(0)()

    raw[...] = jnp.full((8, 128), 1000, jnp.int32)
    raw[0:1, 0:TILES] = rels_in[...] * ROWS + rows_in[...]
    raw[1:2, 0:TILES] = sources_in[...]
    raw[2:3, 0:TILES] = rows_in[...]
    raw[3:4, 0:TILES] = rels_in[...]
    raw[4:5, 0:N_ENT] = needed_in[...]
    lane = lax.broadcasted_iota(jnp.int32, (128, 128), 1)
    line = lax.broadcasted_iota(jnp.int32, (128, 128), 0)

    def turn(i):
        return jnp.broadcast_to(raw[i : i + 1, :], (128, 128)).T

    wanted = jnp.sum(jnp.where(lane == turn(1), jnp.broadcast_to(raw[4:5, :], (128, 128)), 0), axis=1, keepdims=True)
    put, keep, upto, some = arranged(raw, 0)
    meta_wide[0:1, :] = put(line)
    meta_wide[1:2, :] = put(turn(1))
    meta_wide[2:3, :] = put(wanted)
    meta_wide[6:7, :] = upto
    keeps_wide[0:1, :] = keep.astype(F32)
    keeps_wide[2:3, :] = some.astype(F32)
    put, keep, upto, some = arranged(raw, 1)
    meta_wide[3:4, :] = put(line)
    meta_wide[4:5, :] = put(turn(2))
    meta_wide[5:6, :] = put(turn(3))
    meta_wide[7:8, :] = upto
    keeps_wide[1:2, :] = keep.astype(F32)
    keeps_wide[3:4, :] = some.astype(F32)
    keeps_wide[4:8, :] = jnp.zeros((4, 128), F32)
    orders = [
        pltpu.make_async_copy(meta_wide, meta, local.at[4]),
        pltpu.make_async_copy(keeps_wide, keeps, local.at[5]),
    ]
    for order in orders:
        order.start()

    def ask(o, carry):
        req_out[o] = jnp.full((8, 128), needed[0, o], jnp.int32)
        return carry

    lax.fori_loop(0, N_ENT, ask, 0)
    req_in[ent] = req_out[ent]
    spread("ent", N_ENT, ent, lambda o: req_out.at[o], req_in, pair_send.at[1], pair_recv.at[1])
    table[ent] = factors[...]
    run[0] = jnp.zeros((BLK, R), F32)
    for order in orders:
        order.wait()
    moves[2].wait()

    def backward(t):
        own = factors[pl.ds(meta[4, t] * 2, 2)].reshape(BLK, R)
        right = dot(tiles[meta[3, t]], own, ((0,), (0,))).astype(BF16)
        return dot(right, cores[meta[5, t]])

    def backward_part(q):
        sorted_sums(run, 16, backward, lambda t: keeps[1, t], q * 16)

    def pack(o):
        return (run[meta[7, o]] * keeps[3, o]).astype(BF16)

    def give(k, carry):
        o = lax.rem(ent + k, N_ENT)
        terms[o] = pack(o)
        send(terms.at[o], landed.at[ent], pair_send.at[5], pair_recv.at[5], {"ent": o}).start()
        return carry

    backward_part(0)
    backward_part(1)
    spread_wait(N_ENT, sys_in, sys_out, pair_send.at[0], pair_recv.at[0])
    sys_row[...] = jnp.sum(sys_in[...], axis=0)
    spread("rel", N_REL, rel, lambda o: sys_row, sys_rows, pair_send.at[3], pair_recv.at[3])
    sys_rows[rel] = sys_row[...]
    steps.pop(0)()
    backward_part(2)
    steps.pop(0)()
    backward_part(3)
    spread_wait(N_REL, sys_rows, sys_row, pair_send.at[3], pair_recv.at[3])
    unit = lax.broadcasted_iota(jnp.int32, (8, R), 0) + ent * 8 == lax.broadcasted_iota(jnp.int32, (8, R), 1)
    sys_all[ent] = jnp.sum(sys_rows[...], axis=0) + jnp.where(unit, ridge_shift, 0.0)
    spread("ent", N_ENT, ent, lambda o: sys_all.at[ent], sys_all, pair_send.at[4], pair_recv.at[4])
    steps.pop(0)()
    landed[ent] = pack(ent)
    given = [1]

    def advance(count):
        if len(steps) > 1:
            steps.pop(0)()
            count = N_ENT if len(steps) == 1 else count
        upto = min(N_ENT, given[0] + count)
        lax.fori_loop(given[0], upto, give, 0)
        given[0] = upto

    for _ in range(3):
        advance(1)
    spread_wait(N_ENT, sys_all, sys_all, pair_send.at[4], pair_recv.at[4])

    system = sys_all[...].reshape(R, R)
    corner[...] = system[:128, :128]
    band[...] = system[:128, 128:]
    start, some_pivots = sweep(corner, spread_column)

    def pivots():
        carry = start()
        for i in range(8):
            advance(1)
            carry = some_pivots(i * 16, 16, carry)

    pivots()
    first = -corner[...]
    ahead = dot(first, band[...], precision=HIGH)
    low = sys_all[pl.ds(16, 16)].reshape(128, R)[:, 128:]
    corner[...] = low - dot(band[...], ahead, ((0,), (0,)), HIGH)
    inverse[pl.ds(0, 128), pl.ds(0, 128)] = first
    band[...] = ahead
    pivots()
    ahead = band[...]
    second = -corner[...]
    mixed = dot(ahead, second, precision=HIGH)
    inverse[pl.ds(0, 128), pl.ds(0, 128)] += dot(mixed, ahead, ((1,), (1,)), HIGH)
    inverse[pl.ds(0, 128), pl.ds(128, 128)] = -mixed
    inverse[pl.ds(128, 128), pl.ds(0, 128)] = -mixed.T
    inverse[pl.ds(128, 128), pl.ds(128, 128)] = second

    for step in steps:
        step()

    def forward(t):
        return dot(tiles[meta[0, t]], table[meta[1, t], pl.ds(meta[2, t] * 2, 2)].reshape(BLK, R))

    sorted_sums(run, TILES, forward, lambda t: keeps[0, t], 0)
    for b in range(ROWS):
        total = jnp.zeros((BLK, R), F32)
        for j in range(REL_DEV):
            g = j * ROWS + b
            summed = (run[meta[6, g]] * keeps[2, g]).astype(BF16)
            total = total + dot(summed, cores[j], ((1,), (1,)))
        ahead_terms[pl.ds(b * 2, 2)] = total.reshape(2, PIECE, R)
    moves[3].wait()
    wide = jnp.broadcast_to(spectrum[...], (R, R))
    weight[...] = 1.0 / (wide * wide.T + ridge_shift)
    spread_wait(N_ENT, req_in, req_out, pair_send.at[1], pair_recv.at[1])
    spread_wait(N_ENT, landed, terms, pair_send.at[5], pair_recv.at[5])

    def landing(q):
        block = q // 2
        chunk = pl.ds(pl.multiple_of(lax.rem(q, 2) * PIECE, PIECE), PIECE)

        def add(o, total):
            return total + jnp.where(jnp.tile(req_in[o], (8, 2)) == block, landed[o, chunk, :].astype(F32), 0.0)

        return lax.fori_loop(0, N_ENT, add, ahead_terms[q])

    def hand_over(k, carry):
        z = lax.rem(rel + k, N_REL)
        numer_out[z] = landing(z).astype(BF16)
        send(numer_out.at[z], numer_in.at[rel], pair_send.at[2], pair_recv.at[2], {"rel": z}).start()
        return carry

    lax.fori_loop(1, N_REL, hand_over, 0)
    numer_in[rel] = jnp.zeros((PIECE, R), BF16)
    mine = landing(rel)
    spread_wait(N_REL, numer_in, numer_out, pair_send.at[2], pair_recv.at[2])
    total = mine + jnp.sum(numer_in[...].astype(F32), axis=0)
    fresh[ent, rel] = dot(total, inverse[...], precision=HIGH).astype(BF16)
    spread("rel", N_REL, rel, lambda o: fresh.at[ent, rel], fresh.at[ent], pair_send.at[6], pair_recv.at[6])
    basis_wide = pieces(basis[...], 2)
    turned = pieces(basis[...].T, 2)
    spread_wait(N_REL, fresh.at[ent], fresh.at[ent], pair_send.at[6], pair_recv.at[6])
    steps = ring_gather(ent, fresh.at[ent], fresh, ring_send.at[1], ring_recv.at[1])
    steps.pop(0)()
    factors_out[...] = fresh[ent].reshape(SLAB, R)
    for step in steps:
        step()

    def latest(t):
        return dot(tiles[meta[0, t]], fresh[meta[1, t], pl.ds(meta[2, t] * 2, 2)].reshape(BLK, R))

    sorted_sums(run, TILES, latest, lambda t: keeps[0, t], 0)
    for j in range(REL_DEV):
        total = jnp.zeros((R, R), F32)
        for b in range(ROWS):
            g = j * ROWS + b
            summed = (run[meta[6, g]] * keeps[2, g]).astype(BF16)
            total = total + dot(fresh[ent, pl.ds(b * 2, 2)].reshape(BLK, R), summed, ((0,), (0,)))
        sum_out[pl.ds(j * 16, 16)] = total.astype(BF16).reshape(16, 16, R)
    spread("ent", N_ENT, ent, lambda o: sum_out.at[o], sum_in, pair_send.at[7], pair_recv.at[7])
    sum_in[ent] = sum_out[ent]
    spread_wait(N_ENT, sum_in, sum_out, pair_send.at[7], pair_recv.at[7])
    sum_all[ent] = jnp.sum(sum_in[...].astype(F32), axis=0).astype(BF16)
    spread("ent", N_ENT, ent, lambda o: sum_all.at[ent], sum_all, pair_send.at[8], pair_recv.at[8])
    spread_wait(N_ENT, sum_all, sum_all, pair_send.at[8], pair_recv.at[8])
    for j in range(REL_DEV):
        projected = sum_all[pl.ds(j * 16, 16)].reshape(R, R)
        half = pieces(dot_pieces([projected], basis_wide), 2)
        rotated = pieces(dot_pieces(turned, half) * weight[...], 2)
        half = pieces(dot_pieces(rotated, turned), 2)
        cores_out[j] = dot_pieces(basis_wide, half)


def shards(tile_vals, tile_row, tile_rel, tile_src, needed, factors, cores, basis, spectrum):
    smem, vmem = pl.BlockSpec(memory_space=pltpu.SMEM), pl.BlockSpec(memory_space=pltpu.VMEM)
    hbm = pl.BlockSpec(memory_space=pl.ANY)
    asked = needed.reshape(1, N_ENT)
    return pl.pallas_call(
        sweep_kernel,
        out_shape=[jax.ShapeDtypeStruct((SLAB, R), BF16), jax.ShapeDtypeStruct((REL_DEV, R, R), F32)],
        in_specs=[vmem] * 4 + [smem] + [hbm] * 4 + [vmem],
        out_specs=[vmem, vmem],
        scratch_shapes=[
            pltpu.VMEM((TILES, BLK, BLK), BF16),
            pltpu.VMEM((N_REL, PIECE, R), BF16),
            pltpu.VMEM((REL_DEV, R, R), BF16),
            pltpu.VMEM((R, R), F32),
            pltpu.VMEM((8, 128), jnp.int32),
            pltpu.VMEM((8, 128), jnp.int32),
            pltpu.VMEM((8, 128), F32),
            pltpu.SMEM((8, 128), jnp.int32),
            pltpu.SMEM((8, 128), F32),
            pltpu.VMEM((N_ENT, N_REL, PIECE, R), BF16),
            pltpu.VMEM((N_ENT, N_REL, PIECE, R), BF16),
            pltpu.VMEM((TILES + 1, BLK, R), F32),
            pltpu.VMEM((N_REL, PIECE, R), F32),
            pltpu.VMEM((N_ENT, BLK, R), BF16),
            pltpu.VMEM((N_ENT, BLK, R), BF16),
            pltpu.VMEM((N_ENT, 8, 128), jnp.int32),
            pltpu.VMEM((N_ENT, 8, 128), jnp.int32),
            pltpu.VMEM((N_ENT, 8, R), F32),
            pltpu.VMEM((N_ENT, 8, R), F32),
            pltpu.VMEM((8, R), F32),
            pltpu.VMEM((N_REL, 8, R), F32),
            pltpu.VMEM((N_ENT, 8, R), F32),
            pltpu.VMEM((128, 128), F32),
            pltpu.VMEM((128, 128), F32),
            pltpu.VMEM((128, 128), F32),
            pltpu.VMEM((R, R), F32),
            pltpu.VMEM((N_REL, PIECE, R), BF16),
            pltpu.VMEM((N_REL, PIECE, R), BF16),
            pltpu.VMEM((R, R), F32),
            pltpu.VMEM((N_ENT, 16, R), BF16),
            pltpu.VMEM((N_ENT, 16, R), BF16),
            pltpu.VMEM((N_ENT, 16, R), BF16),
            pltpu.SemaphoreType.DMA((2,)),
            pltpu.SemaphoreType.DMA((2, 2, N_ENT)),
            pltpu.SemaphoreType.DMA((9,)),
            pltpu.SemaphoreType.DMA((9,)),
            pltpu.SemaphoreType.DMA((6,)),
        ],
        compiler_params=pltpu.CompilerParams(collective_id=0, has_side_effects=True, vmem_limit_bytes=58 << 20),
        name="sweep",
    )(
        tile_row[0],
        tile_rel[0],
        tile_src[0],
        asked,
        asked,
        tile_vals[0, 0],
        factors.reshape(N_REL, PIECE, R),
        cores,
        basis,
        spectrum.reshape(1, R),
    )


def solution(mesh):
    in_specs = (
        P("ent", "rel", None, None, None),
        P("ent", "rel", None),
        P("ent", "rel", None),
        P("ent", "rel", None),
        P("ent", "rel", None, None),
        P("ent", None),
        P("rel", None, None),
        P(),
        P(),
    )
    out_specs = (P("ent", None), P("rel", None, None))
    return jax.shard_map(
        lambda *args: tuple(shards(*args)), mesh=mesh, in_specs=in_specs, out_specs=out_specs, check_vma=False
    )
```

```python
import functools
import jax
import jax.numpy as jnp
from jax import lax
from jax.experimental import pallas as pl
from jax.experimental.pallas import tpu as pltpu
from jax.sharding import PartitionSpec as P

ridge_shift = 1.0
N_ENT, N_REL = 32, 8
BLK, R, ROWS, TILES, REL_DEV, SLAB = 128, 256, 4, 64, 2, 512
PIECE = SLAB // N_REL
EARLY = N_ENT // 2
MESH = pl.DeviceIdType.MESH
F32, BF16 = jnp.float32, jnp.bfloat16
HIGH = lax.Precision.HIGHEST
SPOT = {0: 0, -1: 1, 1: 2, 2: 3}


def dot(a, b, dims=((1,), (0,)), precision=None):
    return lax.dot_general(a, b, (dims, ((), ())), precision=precision, preferred_element_type=F32)


def send(src, dst, send_sem, recv_sem, target):
    return pltpu.make_async_remote_copy(
        src_ref=src, dst_ref=dst, send_sem=send_sem, recv_sem=recv_sem, device_id=target, device_id_type=MESH
    )


def wait_bytes(ref, sem):
    pltpu.make_async_copy(ref, ref, sem).wait()


def greet(me_ent, me_rel):
    barrier = pltpu.get_barrier_semaphore()

    def ent_signal(k, carry):
        pl.semaphore_signal(barrier, inc=1, device_id={"ent": lax.rem(me_ent + k, N_ENT)}, device_id_type=MESH)
        return carry

    def rel_signal(k, carry):
        pl.semaphore_signal(barrier, inc=1, device_id={"rel": lax.rem(me_rel + k, N_REL)}, device_id_type=MESH)
        return carry

    lax.fori_loop(1, N_ENT, ent_signal, 0)
    lax.fori_loop(1, N_REL, rel_signal, 0)
    return lambda: pl.semaphore_wait(barrier, N_ENT + N_REL - 2)


def pieces(wide, count):
    out = []
    for _ in range(count):
        out.append(wide.astype(BF16))
        wide = wide - out[-1].astype(F32)
    return out


def dot_pieces(left, right, dims=((1,), (0,))):
    longest = max(len(left), len(right))
    terms = [(i + k, dot(a, b, dims)) for i, a in enumerate(left) for k, b in enumerate(right) if i + k < longest]
    return sum(t for _, t in sorted(terms, key=lambda p: -p[0]))


def spread(axis, count, me, source_at, landing, send_sem, recv_sem):
    def one(k, carry):
        other = lax.rem(me + k, count)
        send(source_at(other), landing.at[me], send_sem, recv_sem, {axis: other}).start()
        return carry

    lax.fori_loop(1, count, one, 0)


def spread_wait(count, landing, source, send_sem, recv_sem):
    wait_bytes(landing.at[pl.ds(0, count - 1)], recv_sem)
    wait_bytes(landing.at[pl.ds(0, count - 1)], send_sem)


def ring_gather(me, own, table, send_sem, recv_sem):
    core = lax.rem(me, 2)
    col = lax.rem(me // 2, 4)
    row = me // 8
    way = 1 - 2 * core
    sibling = me + way

    def at(h, u, v):
        du, dv = (u, v) if h == 0 else (v, u)
        x = lax.rem(col + du * way + 8, 4)
        y = lax.rem(row + dv * way + 8, 4)
        return (y * 4 + x) * 2 + core

    def part(ref, h):
        return ref.at[pl.ds(h * N_REL // 2, N_REL // 2)]

    def go(h, u, v, target):
        slab = at(h, u, v)
        dst = part(table.at[slab], h)
        src = part(own, h) if (u, v) == (0, 0) else dst
        send(src, dst, send_sem, recv_sem.at[h, slab], {"ent": target}).start()

    def arrive(h, slab):
        dst = part(table.at[slab], h)
        pltpu.make_async_copy(dst, dst, recv_sem.at[h, slab]).wait()

    def first(h):
        go(h, 0, 0, at(h, 1, 0))
        go(h, 0, 0, at(h, -1, 0))
        go(h, 0, 0, at(h, 0, 1))
        go(h, 0, 0, at(h, 0, -1))
        go(h, 0, 0, sibling)

    def along_u(h, u):
        arrive(h, at(h, u, 0))
        if u == -1:
            go(h, u, 0, at(h, 1, 0))
        go(h, u, 0, at(h, 0, 1))
        go(h, u, 0, at(h, 0, -1))
        go(h, u, 0, sibling)

    def along_v(h, u, v):
        arrive(h, at(h, u, v))
        if v == -1:
            go(h, u, v, at(h, 0, 1))
        go(h, u, v, sibling)

    def both(act, *where):
        return lambda: [act(h, *where) for h in (0, 1)]

    steps = [both(first), both(along_u, -1), both(along_u, 1), both(along_v, 0, -1), both(along_v, 0, 1), both(along_u, 2)]
    for u in (-1, 1):
        steps += [both(along_v, u, -1), both(along_v, u, 1)]
    steps += [both(along_v, 0, 2), both(along_v, 2, -1), both(along_v, 2, 1)]
    steps += [both(along_v, u, 2) for u in (-1, 1, 2)]

    def finish():
        def one(k, carry):
            slab = 2 * k + 1 - core
            arrive(0, slab)
            arrive(1, slab)
            return carry

        lax.fori_loop(0, N_ENT // 2, one, 0)
        wait_bytes(table.at[pl.ds(0, N_ENT - 1)], send_sem)

    return steps + [finish]


def sweep(ref, spread_column):
    size = ref.shape[0]
    rows = lax.broadcasted_iota(jnp.int32, (size, size), 0)
    lanes = lax.broadcasted_iota(jnp.int32, (size, size), 1)
    lane1 = lax.broadcasted_iota(jnp.int32, (1, size), 1)

    def column_of(whole, k):
        return jnp.broadcast_to(jnp.sum(jnp.where(lanes == k, whole, 0.0), axis=1, keepdims=True), (size, size))

    def pivot(k, column, line):
        whole = ref[...]
        later = jnp.minimum(k + 1, size - 1)
        next_column = column_of(whole, k + 1)
        next_line = ref[pl.ds(later, 1), :]
        spread_column[...] = column
        scale = 1.0 / spread_column[pl.ds(k, 1), :]
        factor = spread_column[pl.ds(later, 1), :]
        line = jnp.where(lane1 == k, -1.0, line) * scale
        column = jnp.where(rows == k, -1.0, column)
        ref[...] = jnp.where((lanes == k) | (rows == k), 0.0, whole) - column * line
        next_column = jnp.where(rows == k, 0.0, next_column) - column * (factor * scale)
        next_line = jnp.where(lane1 == k, 0.0, next_line) - factor * line
        return next_column, next_line

    def start():
        return column_of(ref[...], 0), ref[0:1, :]

    def some(k, count, carry):
        def four(q, carry):
            for i in range(4):
                carry = pivot(k + q * 4 + i, *carry)
            return carry

        return lax.fori_loop(0, count // 4, four, carry)

    return start, some


def sorted_sums(run, count, term, keep_at, start):
    def four(q, carry):
        for i in range(4):
            t = start + q * 4 + i
            run[t + 1] = run[t] * keep_at(t) + term(t)
        return carry

    lax.fori_loop(0, count // 4, four, 0)


def arranged(raw, key):
    shape = (128, 128)
    lane = lax.broadcasted_iota(jnp.int32, shape, 1)
    keys = jnp.broadcast_to(raw[key : key + 1, :], shape)
    turned = keys.T
    earlier = (keys == turned) & (lane < lax.broadcasted_iota(jnp.int32, shape, 0))
    rank = jnp.sum(jnp.where((keys < turned) | earlier, 1, 0), axis=1, keepdims=True)
    repeats = jnp.sum(jnp.where(earlier, 1, 0), axis=1, keepdims=True)
    here = rank == lane

    def put(values):
        return jnp.sum(jnp.where(here, values, 0), axis=0, keepdims=True)

    keep = put(jnp.where(repeats > 0, 1, 0))
    upto = jnp.sum(jnp.where(turned <= lane, 1, 0), axis=0, keepdims=True)
    some = jnp.minimum(jnp.sum(jnp.where(turned == lane, 1, 0), axis=0, keepdims=True), 1)
    return put, keep, upto, some


def sweep_kernel(
    rows_in, rels_in, sources_in, needed_in, needed, tiles_hbm, factors_hbm, cores_hbm, basis_hbm, spectrum,
    factors_out, cores_out,
    tiles, factors, cores, basis, raw, meta_wide, keeps_wide, meta, keeps,
    table, fresh, run, ahead_terms, terms, landed, req_out, req_in, sys_out, sys_in, sys_row, sys_rows, sys_all,
    corner, spread_column, band, inverse, numer_out, numer_in, weight, sum_out, sum_in, sum_all,
    ring_send, ring_recv, pair_send, pair_recv, local,
):
    ent = lax.axis_index("ent")
    rel = lax.axis_index("rel")
    all_here = greet(ent, rel)
    moves = [
        pltpu.make_async_copy(a, b, local.at[i])
        for i, (a, b) in enumerate(
            ((factors_hbm, factors), (cores_hbm, cores), (tiles_hbm, tiles), (basis_hbm, basis))
        )
    ]
    for move in moves:
        move.start()

    moves[0].wait()
    moves[1].wait()
    slab_rows = factors[...].reshape(SLAB, R)
    gram = pieces(dot(slab_rows, slab_rows, ((0,), (0,))), 3)
    share = jnp.zeros((R, R), F32)
    for j in range(REL_DEV):
        left = pieces(dot_pieces([cores[j]], gram), 3)
        share = share + dot_pieces(left, [cores[j]], ((1,), (1,)))
        right = pieces(dot_pieces(gram, [cores[j]]), 3)
        share = share + dot_pieces([cores[j]], right, ((0,), (0,)))
    sys_out[...] = share.reshape(N_ENT, 8, R)
    all_here()
    spread("ent", N_ENT, ent, lambda o: sys_out.at[o], sys_in, pair_send.at[0], pair_recv.at[0])
    sys_in[ent] = sys_out[ent]
    steps = ring_gather(ent, factors, table, ring_send.at[0], ring_recv.at[0])
    steps.pop(0)()

    raw[...] = jnp.full((8, 128), 1000, jnp.int32)
    raw[0:1, 0:TILES] = rels_in[...] * ROWS + rows_in[...]
    raw[1:2, 0:TILES] = sources_in[...]
    raw[2:3, 0:TILES] = rows_in[...]
    raw[3:4, 0:TILES] = rels_in[...]
    raw[4:5, 0:N_ENT] = needed_in[...]
    lane = lax.broadcasted_iota(jnp.int32, (128, 128), 1)
    line = lax.broadcasted_iota(jnp.int32, (128, 128), 0)

    def turn(i):
        return jnp.broadcast_to(raw[i : i + 1, :], (128, 128)).T

    wanted = jnp.sum(jnp.where(lane == turn(1), jnp.broadcast_to(raw[4:5, :], (128, 128)), 0), axis=1, keepdims=True)
    put, keep, upto, some = arranged(raw, 0)
    meta_wide[0:1, :] = put(line)
    meta_wide[1:2, :] = put(turn(1))
    meta_wide[2:3, :] = put(wanted)
    meta_wide[6:7, :] = upto
    keeps_wide[0:1, :] = keep.astype(F32)
    keeps_wide[2:3, :] = some.astype(F32)
    put, keep, upto, some = arranged(raw, 1)
    meta_wide[3:4, :] = put(line)
    meta_wide[4:5, :] = put(turn(2))
    meta_wide[5:6, :] = put(turn(3))
    meta_wide[7:8, :] = upto
    keeps_wide[1:2, :] = keep.astype(F32)
    keeps_wide[3:4, :] = some.astype(F32)
    keeps_wide[4:8, :] = jnp.zeros((4, 128), F32)
    orders = [
        pltpu.make_async_copy(meta_wide, meta, local.at[4]),
        pltpu.make_async_copy(keeps_wide, keeps, local.at[5]),
    ]
    for order in orders:
        order.start()

    def ask(o, carry):
        req_out[o] = jnp.full((1, 128), needed[0, o], jnp.int32)
        return carry

    lax.fori_loop(0, N_ENT, ask, 0)
    req_in[ent] = req_out[ent]
    spread("ent", N_ENT, ent, lambda o: req_out.at[o], req_in, pair_send.at[1], pair_recv.at[1])
    table[ent] = factors[...]
    run[0] = jnp.zeros((BLK, R), F32)
    for order in orders:
        order.wait()
    moves[2].wait()

    def backward(t):
        own = factors[pl.ds(meta[4, t] * 2, 2)].reshape(BLK, R)
        right = dot(tiles[meta[3, t]], own, ((0,), (0,))).astype(BF16)
        return dot(right, cores[meta[5, t]])

    def backward_part(q):
        sorted_sums(run, 16, backward, lambda t: keeps[1, t], q * 16)

    def pack(o):
        return (run[meta[7, o]] * keeps[3, o]).astype(BF16)

    def giver(group):
        def give(k, carry):
            o = lax.rem(ent + k, N_ENT)
            terms[o] = pack(o)
            send(terms.at[o], landed.at[ent], pair_send.at[group], pair_recv.at[group], {"ent": o}).start()
            return carry

        return give

    backward_part(0)
    backward_part(1)
    spread_wait(N_ENT, sys_in, sys_out, pair_send.at[0], pair_recv.at[0])
    sys_row[...] = jnp.sum(sys_in[...], axis=0)
    spread("rel", N_REL, rel, lambda o: sys_row, sys_rows, pair_send.at[3], pair_recv.at[3])
    sys_rows[rel] = sys_row[...]
    steps.pop(0)()
    backward_part(2)
    steps.pop(0)()
    backward_part(3)
    spread_wait(N_REL, sys_rows, sys_row, pair_send.at[3], pair_recv.at[3])
    unit = lax.broadcasted_iota(jnp.int32, (8, R), 0) + ent * 8 == lax.broadcasted_iota(jnp.int32, (8, R), 1)
    sys_all[ent] = jnp.sum(sys_rows[...], axis=0) + jnp.where(unit, ridge_shift, 0.0)
    spread("ent", N_ENT, ent, lambda o: sys_all.at[ent], sys_all, pair_send.at[4], pair_recv.at[4])
    steps.pop(0)()
    landed[ent] = pack(ent)
    given = [1]

    def advance(count):
        if len(steps) > 1:
            steps.pop(0)()
            count = N_ENT if len(steps) == 1 else count
        upto = min(N_ENT, given[0] + count)
        middle = min(max(given[0], EARLY), upto)
        lax.fori_loop(given[0], middle, giver(5), 0)
        lax.fori_loop(middle, upto, giver(9), 0)
        given[0] = upto

    for _ in range(3):
        advance(2)
    spread_wait(N_ENT, sys_all, sys_all, pair_send.at[4], pair_recv.at[4])

    system = sys_all[...].reshape(R, R)
    corner[...] = system[:128, :128]
    band[...] = system[:128, 128:]
    start, some_pivots = sweep(corner, spread_column)

    def pivots():
        carry = start()
        for i in range(8):
            advance(2)
            carry = some_pivots(i * 16, 16, carry)

    pivots()
    first = -corner[...]
    ahead = dot(first, band[...], precision=HIGH)
    low = sys_all[pl.ds(16, 16)].reshape(128, R)[:, 128:]
    corner[...] = low - dot(band[...], ahead, ((0,), (0,)), HIGH)
    inverse[pl.ds(0, 128), pl.ds(0, 128)] = first
    band[...] = ahead
    pivots()
    ahead = band[...]
    second = -corner[...]
    mixed = dot(ahead, second, precision=HIGH)
    inverse[pl.ds(0, 128), pl.ds(0, 128)] += dot(mixed, ahead, ((1,), (1,)), HIGH)
    inverse[pl.ds(0, 128), pl.ds(128, 128)] = -mixed
    inverse[pl.ds(128, 128), pl.ds(0, 128)] = -mixed.T
    inverse[pl.ds(128, 128), pl.ds(128, 128)] = second

    for step in steps:
        step()

    def forward(t):
        return dot(tiles[meta[0, t]], table[meta[1, t], pl.ds(meta[2, t] * 2, 2)].reshape(BLK, R))

    sorted_sums(run, TILES, forward, lambda t: keeps[0, t], 0)
    for b in range(ROWS):
        total = jnp.zeros((BLK, R), F32)
        for j in range(REL_DEV):
            g = j * ROWS + b
            summed = (run[meta[6, g]] * keeps[2, g]).astype(BF16)
            total = total + dot(summed, cores[j], ((1,), (1,)))
        ahead_terms[pl.ds(b * 2, 2)] = total.reshape(2, PIECE, R)
    moves[3].wait()
    wide = jnp.broadcast_to(spectrum[...], (R, R))
    weight[...] = 1.0 / (wide * wide.T + ridge_shift)
    spread_wait(N_ENT, req_in, req_out, pair_send.at[1], pair_recv.at[1])
    spread_wait(EARLY, landed, terms, pair_send.at[5], pair_recv.at[5])

    def landing(q, least, most, total):
        block = q // 2
        chunk = pl.ds(pl.multiple_of(lax.rem(q, 2) * PIECE, PIECE), PIECE)

        def add(k, total):
            o = lax.rem(ent - k + N_ENT, N_ENT)
            asked = jnp.broadcast_to(jnp.concatenate([req_in[o]] * 2, axis=1), (PIECE, R))
            return total + jnp.where(asked == block, landed[o, chunk, :].astype(F32), 0.0)

        return lax.fori_loop(least, most, add, total)

    def early(q, carry):
        ahead_terms[q] = landing(q, 0, EARLY, ahead_terms[q])
        return carry

    lax.fori_loop(0, N_REL, early, 0)
    spread_wait(N_ENT - EARLY + 1, landed, terms, pair_send.at[9], pair_recv.at[9])

    def hand_over(k, carry):
        z = lax.rem(rel + k, N_REL)
        numer_out[z] = landing(z, EARLY, N_ENT, ahead_terms[z]).astype(BF16)
        send(numer_out.at[z], numer_in.at[rel], pair_send.at[2], pair_recv.at[2], {"rel": z}).start()
        return carry

    lax.fori_loop(1, N_REL, hand_over, 0)
    numer_in[rel] = jnp.zeros((PIECE, R), BF16)
    mine = landing(rel, EARLY, N_ENT, ahead_terms[rel])
    spread_wait(N_REL, numer_in, numer_out, pair_send.at[2], pair_recv.at[2])
    total = mine + jnp.sum(numer_in[...].astype(F32), axis=0)
    fresh[ent, rel] = dot(total, inverse[...], precision=HIGH).astype(BF16)
    spread("rel", N_REL, rel, lambda o: fresh.at[ent, rel], fresh.at[ent], pair_send.at[6], pair_recv.at[6])
    basis_wide = pieces(basis[...], 2)
    turned = pieces(basis[...].T, 2)
    spread_wait(N_REL, fresh.at[ent], fresh.at[ent], pair_send.at[6], pair_recv.at[6])
    steps = ring_gather(ent, fresh.at[ent], fresh, ring_send.at[1], ring_recv.at[1])
    steps.pop(0)()
    factors_out[...] = fresh[ent].reshape(SLAB, R)
    for step in steps:
        step()

    def latest(t):
        return dot(tiles[meta[0, t]], fresh[meta[1, t], pl.ds(meta[2, t] * 2, 2)].reshape(BLK, R))

    sorted_sums(run, TILES, latest, lambda t: keeps[0, t], 0)
    for j in range(REL_DEV):
        total = jnp.zeros((R, R), F32)
        for b in range(ROWS):
            g = j * ROWS + b
            summed = (run[meta[6, g]] * keeps[2, g]).astype(BF16)
            total = total + dot(fresh[ent, pl.ds(b * 2, 2)].reshape(BLK, R), summed, ((0,), (0,)))
        sum_out[pl.ds(j * 16, 16)] = total.astype(BF16).reshape(16, 16, R)
    spread("ent", N_ENT, ent, lambda o: sum_out.at[o], sum_in, pair_send.at[7], pair_recv.at[7])
    sum_in[ent] = sum_out[ent]
    spread_wait(N_ENT, sum_in, sum_out, pair_send.at[7], pair_recv.at[7])
    sum_all[ent] = jnp.sum(sum_in[...].astype(F32), axis=0).astype(BF16)
    spread("ent", N_ENT, ent, lambda o: sum_all.at[ent], sum_all, pair_send.at[8], pair_recv.at[8])
    spread_wait(N_ENT, sum_all, sum_all, pair_send.at[8], pair_recv.at[8])
    for j in range(REL_DEV):
        projected = sum_all[pl.ds(j * 16, 16)].reshape(R, R)
        half = pieces(dot_pieces([projected], basis_wide), 2)
        rotated = pieces(dot_pieces(turned, half) * weight[...], 2)
        half = pieces(dot_pieces(rotated, turned), 2)
        cores_out[j] = dot_pieces(basis_wide, half)


def shards(tile_vals, tile_row, tile_rel, tile_src, needed, factors, cores, basis, spectrum):
    smem, vmem = pl.BlockSpec(memory_space=pltpu.SMEM), pl.BlockSpec(memory_space=pltpu.VMEM)
    hbm = pl.BlockSpec(memory_space=pl.ANY)
    asked = needed.reshape(1, N_ENT)
    return pl.pallas_call(
        sweep_kernel,
        out_shape=[jax.ShapeDtypeStruct((SLAB, R), BF16), jax.ShapeDtypeStruct((REL_DEV, R, R), F32)],
        in_specs=[vmem] * 4 + [smem] + [hbm] * 4 + [vmem],
        out_specs=[vmem, vmem],
        scratch_shapes=[
            pltpu.VMEM((TILES, BLK, BLK), BF16),
            pltpu.VMEM((N_REL, PIECE, R), BF16),
            pltpu.VMEM((REL_DEV, R, R), BF16),
            pltpu.VMEM((R, R), F32),
            pltpu.VMEM((8, 128), jnp.int32),
            pltpu.VMEM((8, 128), jnp.int32),
            pltpu.VMEM((8, 128), F32),
            pltpu.SMEM((8, 128), jnp.int32),
            pltpu.SMEM((8, 128), F32),
            pltpu.VMEM((N_ENT, N_REL, PIECE, R), BF16),
            pltpu.VMEM((N_ENT, N_REL, PIECE, R), BF16),
            pltpu.VMEM((TILES + 1, BLK, R), F32),
            pltpu.VMEM((N_REL, PIECE, R), F32),
            pltpu.VMEM((N_ENT, BLK, R), BF16),
            pltpu.VMEM((N_ENT, BLK, R), BF16),
            pltpu.VMEM((N_ENT, 1, 128), jnp.int32),
            pltpu.VMEM((N_ENT, 1, 128), jnp.int32),
            pltpu.VMEM((N_ENT, 8, R), F32),
            pltpu.VMEM((N_ENT, 8, R), F32),
            pltpu.VMEM((8, R), F32),
            pltpu.VMEM((N_REL, 8, R), F32),
            pltpu.VMEM((N_ENT, 8, R), F32),
            pltpu.VMEM((128, 128), F32),
            pltpu.VMEM((128, 128), F32),
            pltpu.VMEM((128, 128), F32),
            pltpu.VMEM((R, R), F32),
            pltpu.VMEM((N_REL, PIECE, R), BF16),
            pltpu.VMEM((N_REL, PIECE, R), BF16),
            pltpu.VMEM((R, R), F32),
            pltpu.VMEM((N_ENT, 16, R), BF16),
            pltpu.VMEM((N_ENT, 16, R), BF16),
            pltpu.VMEM((N_ENT, 16, R), BF16),
            pltpu.SemaphoreType.DMA((2,)),
            pltpu.SemaphoreType.DMA((2, 2, N_ENT)),
            pltpu.SemaphoreType.DMA((10,)),
            pltpu.SemaphoreType.DMA((10,)),
            pltpu.SemaphoreType.DMA((6,)),
        ],
        compiler_params=pltpu.CompilerParams(collective_id=0, has_side_effects=True, vmem_limit_bytes=58 << 20),
        name="sweep",
    )(
        tile_row[0],
        tile_rel[0],
        tile_src[0],
        asked,
        asked,
        tile_vals[0, 0],
        factors.reshape(N_REL, PIECE, R),
        cores,
        basis,
        spectrum.reshape(1, R),
    )


def solution(mesh):
    in_specs = (
        P("ent", "rel", None, None, None),
        P("ent", "rel", None),
        P("ent", "rel", None),
        P("ent", "rel", None),
        P("ent", "rel", None, None),
        P("ent", None),
        P("rel", None, None),
        P(),
        P(),
    )
    out_specs = (P("ent", None), P("rel", None, None))
    return jax.shard_map(
        lambda *args: tuple(shards(*args)), mesh=mesh, in_specs=in_specs, out_specs=out_specs, check_vma=False
    )
```

```python
import functools
import jax
import jax.numpy as jnp
from jax import lax
from jax.experimental import pallas as pl
from jax.experimental.pallas import tpu as pltpu
from jax.sharding import PartitionSpec as P

ridge_shift = 1.0
N_ENT, N_REL = 32, 8
BLK, R, ROWS, TILES, REL_DEV, SLAB = 128, 256, 4, 64, 2, 512
PIECE = SLAB // N_REL
EARLY = N_ENT // 2
MESH = pl.DeviceIdType.MESH
F32, BF16 = jnp.float32, jnp.bfloat16
HIGH = lax.Precision.HIGHEST
SPOT = {0: 0, -1: 1, 1: 2, 2: 3}


def dot(a, b, dims=((1,), (0,)), precision=None):
    return lax.dot_general(a, b, (dims, ((), ())), precision=precision, preferred_element_type=F32)


def send(src, dst, send_sem, recv_sem, target):
    return pltpu.make_async_remote_copy(
        src_ref=src, dst_ref=dst, send_sem=send_sem, recv_sem=recv_sem, device_id=target, device_id_type=MESH
    )


def wait_bytes(ref, sem):
    pltpu.make_async_copy(ref, ref, sem).wait()


def greet(me_ent, me_rel):
    barrier = pltpu.get_barrier_semaphore()

    def ent_signal(k, carry):
        pl.semaphore_signal(barrier, inc=1, device_id={"ent": lax.rem(me_ent + k, N_ENT)}, device_id_type=MESH)
        return carry

    def rel_signal(k, carry):
        pl.semaphore_signal(barrier, inc=1, device_id={"rel": lax.rem(me_rel + k, N_REL)}, device_id_type=MESH)
        return carry

    lax.fori_loop(1, N_ENT, ent_signal, 0)
    lax.fori_loop(1, N_REL, rel_signal, 0)
    return lambda: pl.semaphore_wait(barrier, N_ENT + N_REL - 2)


def pieces(wide, count):
    out = []
    for _ in range(count):
        out.append(wide.astype(BF16))
        wide = wide - out[-1].astype(F32)
    return out


def dot_pieces(left, right, dims=((1,), (0,))):
    longest = max(len(left), len(right))
    terms = [(i + k, dot(a, b, dims)) for i, a in enumerate(left) for k, b in enumerate(right) if i + k < longest]
    return sum(t for _, t in sorted(terms, key=lambda p: -p[0]))


def spread(axis, count, me, source_at, landing, send_sem, recv_sem):
    def one(k, carry):
        other = lax.rem(me + k, count)
        send(source_at(other), landing.at[me], send_sem, recv_sem, {axis: other}).start()
        return carry

    lax.fori_loop(1, count, one, 0)


def spread_wait(count, landing, source, send_sem, recv_sem):
    wait_bytes(landing.at[pl.ds(0, count - 1)], recv_sem)
    wait_bytes(landing.at[pl.ds(0, count - 1)], send_sem)


def ring_gather(me, own, table, send_sem, recv_sem):
    core = lax.rem(me, 2)
    col = lax.rem(me // 2, 4)
    row = me // 8
    way = 1 - 2 * core
    sibling = me + way

    def at(h, u, v):
        du, dv = (u, v) if h == 0 else (v, u)
        x = lax.rem(col + du * way + 8, 4)
        y = lax.rem(row + dv * way + 8, 4)
        return (y * 4 + x) * 2 + core

    def part(ref, h):
        return ref.at[pl.ds(h * N_REL // 2, N_REL // 2)]

    def go(h, u, v, target):
        slab = at(h, u, v)
        dst = part(table.at[slab], h)
        src = part(own, h) if (u, v) == (0, 0) else dst
        send(src, dst, send_sem, recv_sem.at[h, slab], {"ent": target}).start()

    def arrive(h, slab):
        dst = part(table.at[slab], h)
        pltpu.make_async_copy(dst, dst, recv_sem.at[h, slab]).wait()

    def first(h):
        go(h, 0, 0, at(h, 1, 0))
        go(h, 0, 0, at(h, -1, 0))
        go(h, 0, 0, at(h, 0, 1))
        go(h, 0, 0, at(h, 0, -1))
        go(h, 0, 0, sibling)

    def along_u(h, u):
        arrive(h, at(h, u, 0))
        if u == -1:
            go(h, u, 0, at(h, 1, 0))
        go(h, u, 0, at(h, 0, 1))
        go(h, u, 0, at(h, 0, -1))
        go(h, u, 0, sibling)

    def along_v(h, u, v):
        arrive(h, at(h, u, v))
        if v == -1:
            go(h, u, v, at(h, 0, 1))
        go(h, u, v, sibling)

    def both(act, *where):
        return lambda: [act(h, *where) for h in (0, 1)]

    steps = [both(first), both(along_u, -1), both(along_u, 1), both(along_v, 0, -1), both(along_v, 0, 1), both(along_u, 2)]
    for u in (-1, 1):
        steps += [both(along_v, u, -1), both(along_v, u, 1)]
    steps += [both(along_v, 0, 2), both(along_v, 2, -1), both(along_v, 2, 1)]
    steps += [both(along_v, u, 2) for u in (-1, 1, 2)]

    def finish():
        def one(k, carry):
            slab = 2 * k + 1 - core
            arrive(0, slab)
            arrive(1, slab)
            return carry

        lax.fori_loop(0, N_ENT // 2, one, 0)
        wait_bytes(table.at[pl.ds(0, N_ENT - 1)], send_sem)

    return steps + [finish]


def sweep(ref, spread_column):
    size = ref.shape[0]
    rows = lax.broadcasted_iota(jnp.int32, (size, size), 0)
    lanes = lax.broadcasted_iota(jnp.int32, (size, size), 1)
    lane1 = lax.broadcasted_iota(jnp.int32, (1, size), 1)

    def column_of(whole, k):
        return jnp.broadcast_to(jnp.sum(jnp.where(lanes == k, whole, 0.0), axis=1, keepdims=True), (size, size))

    def pivot(k, column, line):
        whole = ref[...]
        later = jnp.minimum(k + 1, size - 1)
        next_column = column_of(whole, k + 1)
        next_line = ref[pl.ds(later, 1), :]
        spread_column[...] = column
        scale = 1.0 / spread_column[pl.ds(k, 1), :]
        factor = spread_column[pl.ds(later, 1), :]
        line = jnp.where(lane1 == k, -1.0, line) * scale
        column = jnp.where(rows == k, -1.0, column)
        ref[...] = jnp.where((lanes == k) | (rows == k), 0.0, whole) - column * line
        next_column = jnp.where(rows == k, 0.0, next_column) - column * (factor * scale)
        next_line = jnp.where(lane1 == k, 0.0, next_line) - factor * line
        return next_column, next_line

    def start():
        return column_of(ref[...], 0), ref[0:1, :]

    def some(k, count, carry):
        def four(q, carry):
            for i in range(4):
                carry = pivot(k + q * 4 + i, *carry)
            return carry

        return lax.fori_loop(0, count // 4, four, carry)

    return start, some


def sorted_sums(run, count, term, keep_at, start):
    def eight(q, carry):
        for i in range(8):
            t = start + q * 8 + i
            run[t + 1] = run[t] * keep_at(t) + term(t)
        return carry

    lax.fori_loop(0, count // 8, eight, 0)


def arranged(raw, key):
    shape = (128, 128)
    lane = lax.broadcasted_iota(jnp.int32, shape, 1)
    keys = jnp.broadcast_to(raw[key : key + 1, :], shape)
    turned = keys.T
    earlier = (keys == turned) & (lane < lax.broadcasted_iota(jnp.int32, shape, 0))
    rank = jnp.sum(jnp.where((keys < turned) | earlier, 1, 0), axis=1, keepdims=True)
    repeats = jnp.sum(jnp.where(earlier, 1, 0), axis=1, keepdims=True)
    here = rank == lane

    def put(values):
        return jnp.sum(jnp.where(here, values, 0), axis=0, keepdims=True)

    keep = put(jnp.where(repeats > 0, 1, 0))
    upto = jnp.sum(jnp.where(turned <= lane, 1, 0), axis=0, keepdims=True)
    some = jnp.minimum(jnp.sum(jnp.where(turned == lane, 1, 0), axis=0, keepdims=True), 1)
    return put, keep, upto, some


def sweep_kernel(
    rows_in, rels_in, sources_in, needed_in, needed, tiles_hbm, factors_hbm, cores_hbm, basis_hbm, spectrum,
    factors_out, cores_out,
    tiles, factors, cores, basis, raw, meta_wide, keeps_wide, meta, keeps,
    table, fresh, run, ahead_terms, terms, landed, req_out, req_in, sys_out, sys_in, sys_row, sys_rows, sys_all,
    corner, spread_column, band, inverse, numer_out, numer_in, weight, sum_out, sum_in, sum_all,
    ring_send, ring_recv, pair_send, pair_recv, local,
):
    ent = lax.axis_index("ent")
    rel = lax.axis_index("rel")
    all_here = greet(ent, rel)
    moves = [
        pltpu.make_async_copy(a, b, local.at[i])
        for i, (a, b) in enumerate(
            ((factors_hbm, factors), (cores_hbm, cores), (tiles_hbm, tiles), (basis_hbm, basis))
        )
    ]
    for move in moves:
        move.start()

    moves[0].wait()
    moves[1].wait()
    slab_rows = factors[...].reshape(SLAB, R)
    gram = pieces(dot(slab_rows, slab_rows, ((0,), (0,))), 3)
    share = jnp.zeros((R, R), F32)
    for j in range(REL_DEV):
        left = pieces(dot_pieces([cores[j]], gram), 3)
        share = share + dot_pieces(left, [cores[j]], ((1,), (1,)))
        right = pieces(dot_pieces(gram, [cores[j]]), 3)
        share = share + dot_pieces([cores[j]], right, ((0,), (0,)))
    sys_out[...] = share.reshape(N_ENT, 8, R)
    all_here()
    spread("ent", N_ENT, ent, lambda o: sys_out.at[o], sys_in, pair_send.at[0], pair_recv.at[0])
    sys_in[ent] = sys_out[ent]
    steps = ring_gather(ent, factors, table, ring_send.at[0], ring_recv.at[0])
    steps.pop(0)()

    raw[...] = jnp.full((8, 128), 1000, jnp.int32)
    raw[0:1, 0:TILES] = rels_in[...] * ROWS + rows_in[...]
    raw[1:2, 0:TILES] = sources_in[...]
    raw[2:3, 0:TILES] = rows_in[...]
    raw[3:4, 0:TILES] = rels_in[...]
    raw[4:5, 0:N_ENT] = needed_in[...]
    lane = lax.broadcasted_iota(jnp.int32, (128, 128), 1)
    line = lax.broadcasted_iota(jnp.int32, (128, 128), 0)

    def turn(i):
        return jnp.broadcast_to(raw[i : i + 1, :], (128, 128)).T

    wanted = jnp.sum(jnp.where(lane == turn(1), jnp.broadcast_to(raw[4:5, :], (128, 128)), 0), axis=1, keepdims=True)
    put, keep, upto, some = arranged(raw, 0)
    meta_wide[0:1, :] = put(line)
    meta_wide[1:2, :] = put(turn(1))
    meta_wide[2:3, :] = put(wanted)
    meta_wide[6:7, :] = upto
    keeps_wide[0:1, :] = keep.astype(F32)
    keeps_wide[2:3, :] = some.astype(F32)
    put, keep, upto, some = arranged(raw, 1)
    meta_wide[3:4, :] = put(line)
    meta_wide[4:5, :] = put(turn(2))
    meta_wide[5:6, :] = put(turn(3))
    meta_wide[7:8, :] = upto
    keeps_wide[1:2, :] = keep.astype(F32)
    keeps_wide[3:4, :] = some.astype(F32)
    keeps_wide[4:8, :] = jnp.zeros((4, 128), F32)
    orders = [
        pltpu.make_async_copy(meta_wide, meta, local.at[4]),
        pltpu.make_async_copy(keeps_wide, keeps, local.at[5]),
    ]
    for order in orders:
        order.start()

    def ask(o, carry):
        req_out[o] = jnp.full((1, 128), needed[0, o], jnp.int32)
        return carry

    lax.fori_loop(0, N_ENT, ask, 0)
    req_in[ent] = req_out[ent]
    spread("ent", N_ENT, ent, lambda o: req_out.at[o], req_in, pair_send.at[1], pair_recv.at[1])
    table[ent] = factors[...]
    run[0] = jnp.zeros((BLK, R), F32)
    for order in orders:
        order.wait()
    moves[2].wait()

    def backward(t):
        own = factors[pl.ds(meta[4, t] * 2, 2)].reshape(BLK, R)
        right = dot(tiles[meta[3, t]], own, ((0,), (0,))).astype(BF16)
        return dot(right, cores[meta[5, t]])

    def backward_part(q):
        sorted_sums(run, 16, backward, lambda t: keeps[1, t], q * 16)

    def pack(o):
        return (run[meta[7, o]] * keeps[3, o]).astype(BF16)

    def giver(group):
        def give(k, carry):
            o = lax.rem(ent + k, N_ENT)
            terms[o] = pack(o)
            send(terms.at[o], landed.at[ent], pair_send.at[group], pair_recv.at[group], {"ent": o}).start()
            return carry

        return give

    backward_part(0)
    backward_part(1)
    spread_wait(N_ENT, sys_in, sys_out, pair_send.at[0], pair_recv.at[0])
    sys_row[...] = jnp.sum(sys_in[...], axis=0)
    spread("rel", N_REL, rel, lambda o: sys_row, sys_rows, pair_send.at[3], pair_recv.at[3])
    sys_rows[rel] = sys_row[...]
    steps.pop(0)()
    backward_part(2)
    steps.pop(0)()
    backward_part(3)
    spread_wait(N_REL, sys_rows, sys_row, pair_send.at[3], pair_recv.at[3])
    unit = lax.broadcasted_iota(jnp.int32, (8, R), 0) + ent * 8 == lax.broadcasted_iota(jnp.int32, (8, R), 1)
    sys_all[ent] = jnp.sum(sys_rows[...], axis=0) + jnp.where(unit, ridge_shift, 0.0)
    spread("ent", N_ENT, ent, lambda o: sys_all.at[ent], sys_all, pair_send.at[4], pair_recv.at[4])
    steps.pop(0)()
    landed[ent] = pack(ent)
    given = [1]

    def advance(count):
        if len(steps) > 1:
            steps.pop(0)()
            count = N_ENT if len(steps) == 1 else count
        upto = min(N_ENT, given[0] + count)
        middle = min(max(given[0], EARLY), upto)
        lax.fori_loop(given[0], middle, giver(5), 0)
        lax.fori_loop(middle, upto, giver(9), 0)
        given[0] = upto

    for _ in range(3):
        advance(2)
    spread_wait(N_ENT, sys_all, sys_all, pair_send.at[4], pair_recv.at[4])

    system = sys_all[...].reshape(R, R)
    corner[...] = system[:128, :128]
    band[...] = system[:128, 128:]
    start, some_pivots = sweep(corner, spread_column)

    def pivots():
        carry = start()
        for i in range(8):
            advance(2)
            carry = some_pivots(i * 16, 16, carry)

    pivots()
    first = -corner[...]
    ahead = dot(first, band[...], precision=HIGH)
    low = sys_all[pl.ds(16, 16)].reshape(128, R)[:, 128:]
    corner[...] = low - dot(band[...], ahead, ((0,), (0,)), HIGH)
    inverse[pl.ds(0, 128), pl.ds(0, 128)] = first
    band[...] = ahead
    pivots()
    ahead = band[...]
    second = -corner[...]
    mixed = dot(ahead, second, precision=HIGH)
    inverse[pl.ds(0, 128), pl.ds(0, 128)] += dot(mixed, ahead, ((1,), (1,)), HIGH)
    inverse[pl.ds(0, 128), pl.ds(128, 128)] = -mixed
    inverse[pl.ds(128, 128), pl.ds(0, 128)] = -mixed.T
    inverse[pl.ds(128, 128), pl.ds(128, 128)] = second

    for step in steps:
        step()

    def forward(t):
        return dot(tiles[meta[0, t]], table[meta[1, t], pl.ds(meta[2, t] * 2, 2)].reshape(BLK, R))

    sorted_sums(run, TILES, forward, lambda t: keeps[0, t], 0)
    for b in range(ROWS):
        total = jnp.zeros((BLK, R), F32)
        for j in range(REL_DEV):
            g = j * ROWS + b
            summed = (run[meta[6, g]] * keeps[2, g]).astype(BF16)
            total = total + dot(summed, cores[j], ((1,), (1,)))
        ahead_terms[pl.ds(b * 2, 2)] = total.reshape(2, PIECE, R)
    moves[3].wait()
    wide = jnp.broadcast_to(spectrum[...], (R, R))
    weight[...] = 1.0 / (wide * wide.T + ridge_shift)
    spread_wait(N_ENT, req_in, req_out, pair_send.at[1], pair_recv.at[1])
    spread_wait(EARLY, landed, terms, pair_send.at[5], pair_recv.at[5])

    def landing(q, least, most, total):
        block = q // 2
        chunk = pl.ds(pl.multiple_of(lax.rem(q, 2) * PIECE, PIECE), PIECE)

        def add(k, total):
            o = lax.rem(ent - k + N_ENT, N_ENT)
            asked = jnp.broadcast_to(jnp.concatenate([req_in[o]] * 2, axis=1), (PIECE, R))
            return total + jnp.where(asked == block, landed[o, chunk, :].astype(F32), 0.0)

        return lax.fori_loop(least, most, add, total)

    def early(q, carry):
        ahead_terms[q] = landing(q, 0, EARLY, ahead_terms[q])
        return carry

    lax.fori_loop(0, N_REL, early, 0)
    spread_wait(N_ENT - EARLY + 1, landed, terms, pair_send.at[9], pair_recv.at[9])

    def hand_over(k, carry):
        z = lax.rem(rel + k, N_REL)
        numer_out[z] = landing(z, EARLY, N_ENT, ahead_terms[z]).astype(BF16)
        send(numer_out.at[z], numer_in.at[rel], pair_send.at[2], pair_recv.at[2], {"rel": z}).start()
        return carry

    lax.fori_loop(1, N_REL, hand_over, 0)
    numer_in[rel] = jnp.zeros((PIECE, R), BF16)
    mine = landing(rel, EARLY, N_ENT, ahead_terms[rel])
    spread_wait(N_REL, numer_in, numer_out, pair_send.at[2], pair_recv.at[2])
    total = mine + jnp.sum(numer_in[...].astype(F32), axis=0)
    fresh[ent, rel] = dot(total, inverse[...], precision=HIGH).astype(BF16)
    spread("rel", N_REL, rel, lambda o: fresh.at[ent, rel], fresh.at[ent], pair_send.at[6], pair_recv.at[6])
    basis_wide = pieces(basis[...], 2)
    turned = pieces(basis[...].T, 2)
    spread_wait(N_REL, fresh.at[ent], fresh.at[ent], pair_send.at[6], pair_recv.at[6])
    steps = ring_gather(ent, fresh.at[ent], fresh, ring_send.at[1], ring_recv.at[1])
    steps.pop(0)()
    factors_out[...] = fresh[ent].reshape(SLAB, R)
    for step in steps:
        step()

    def latest(t):
        return dot(tiles[meta[0, t]], fresh[meta[1, t], pl.ds(meta[2, t] * 2, 2)].reshape(BLK, R))

    sorted_sums(run, TILES, latest, lambda t: keeps[0, t], 0)
    for j in range(REL_DEV):
        total = jnp.zeros((R, R), F32)
        for b in range(ROWS):
            g = j * ROWS + b
            summed = (run[meta[6, g]] * keeps[2, g]).astype(BF16)
            total = total + dot(fresh[ent, pl.ds(b * 2, 2)].reshape(BLK, R), summed, ((0,), (0,)))
        sum_out[pl.ds(j * 16, 16)] = total.astype(BF16).reshape(16, 16, R)
    spread("ent", N_ENT, ent, lambda o: sum_out.at[o], sum_in, pair_send.at[7], pair_recv.at[7])
    sum_in[ent] = sum_out[ent]
    spread_wait(N_ENT, sum_in, sum_out, pair_send.at[7], pair_recv.at[7])
    sum_all[ent] = jnp.sum(sum_in[...].astype(F32), axis=0).astype(BF16)
    spread("ent", N_ENT, ent, lambda o: sum_all.at[ent], sum_all, pair_send.at[8], pair_recv.at[8])
    spread_wait(N_ENT, sum_all, sum_all, pair_send.at[8], pair_recv.at[8])
    for j in range(REL_DEV):
        projected = sum_all[pl.ds(j * 16, 16)].reshape(R, R)
        half = pieces(dot_pieces([projected], basis_wide), 2)
        rotated = pieces(dot_pieces(turned, half) * weight[...], 2)
        half = pieces(dot_pieces(rotated, turned), 2)
        cores_out[j] = dot_pieces(basis_wide, half)


def shards(tile_vals, tile_row, tile_rel, tile_src, needed, factors, cores, basis, spectrum):
    smem, vmem = pl.BlockSpec(memory_space=pltpu.SMEM), pl.BlockSpec(memory_space=pltpu.VMEM)
    hbm = pl.BlockSpec(memory_space=pl.ANY)
    asked = needed.reshape(1, N_ENT)
    return pl.pallas_call(
        sweep_kernel,
        out_shape=[jax.ShapeDtypeStruct((SLAB, R), BF16), jax.ShapeDtypeStruct((REL_DEV, R, R), F32)],
        in_specs=[vmem] * 4 + [smem] + [hbm] * 4 + [vmem],
        out_specs=[vmem, vmem],
        scratch_shapes=[
            pltpu.VMEM((TILES, BLK, BLK), BF16),
            pltpu.VMEM((N_REL, PIECE, R), BF16),
            pltpu.VMEM((REL_DEV, R, R), BF16),
            pltpu.VMEM((R, R), F32),
            pltpu.VMEM((8, 128), jnp.int32),
            pltpu.VMEM((8, 128), jnp.int32),
            pltpu.VMEM((8, 128), F32),
            pltpu.SMEM((8, 128), jnp.int32),
            pltpu.SMEM((8, 128), F32),
            pltpu.VMEM((N_ENT, N_REL, PIECE, R), BF16),
            pltpu.VMEM((N_ENT, N_REL, PIECE, R), BF16),
            pltpu.VMEM((TILES + 1, BLK, R), F32),
            pltpu.VMEM((N_REL, PIECE, R), F32),
            pltpu.VMEM((N_ENT, BLK, R), BF16),
            pltpu.VMEM((N_ENT, BLK, R), BF16),
            pltpu.VMEM((N_ENT, 1, 128), jnp.int32),
            pltpu.VMEM((N_ENT, 1, 128), jnp.int32),
            pltpu.VMEM((N_ENT, 8, R), F32),
            pltpu.VMEM((N_ENT, 8, R), F32),
            pltpu.VMEM((8, R), F32),
            pltpu.VMEM((N_REL, 8, R), F32),
            pltpu.VMEM((N_ENT, 8, R), F32),
            pltpu.VMEM((128, 128), F32),
            pltpu.VMEM((128, 128), F32),
            pltpu.VMEM((128, 128), F32),
            pltpu.VMEM((R, R), F32),
            pltpu.VMEM((N_REL, PIECE, R), BF16),
            pltpu.VMEM((N_REL, PIECE, R), BF16),
            pltpu.VMEM((R, R), F32),
            pltpu.VMEM((N_ENT, 16, R), BF16),
            pltpu.VMEM((N_ENT, 16, R), BF16),
            pltpu.VMEM((N_ENT, 16, R), BF16),
            pltpu.SemaphoreType.DMA((2,)),
            pltpu.SemaphoreType.DMA((2, 2, N_ENT)),
            pltpu.SemaphoreType.DMA((10,)),
            pltpu.SemaphoreType.DMA((10,)),
            pltpu.SemaphoreType.DMA((6,)),
        ],
        compiler_params=pltpu.CompilerParams(collective_id=0, has_side_effects=True, vmem_limit_bytes=58 << 20),
        name="sweep",
    )(
        tile_row[0],
        tile_rel[0],
        tile_src[0],
        asked,
        asked,
        tile_vals[0, 0],
        factors.reshape(N_REL, PIECE, R),
        cores,
        basis,
        spectrum.reshape(1, R),
    )


def solution(mesh):
    in_specs = (
        P("ent", "rel", None, None, None),
        P("ent", "rel", None),
        P("ent", "rel", None),
        P("ent", "rel", None),
        P("ent", "rel", None, None),
        P("ent", None),
        P("rel", None, None),
        P(),
        P(),
    )
    out_specs = (P("ent", None), P("rel", None, None))
    return jax.shard_map(
        lambda *args: tuple(shards(*args)), mesh=mesh, in_specs=in_specs, out_specs=out_specs, check_vma=False
    )
```
